256 devices in a mesh: row: 16 (over z, core), blk: 16 (over y, x).
Axes of the slice: x: 4, y: 4, z: 8, core: 2. Of those that a mesh axis runs over, the one named last changes fastest.
Arguments:
- tiles: bfloat16 [16, 16, 32, 256, 256], P('row', 'blk')
- tile_rows: int32 [16, 16, 32], P('row', 'blk'), may hold values from 0 to 15, as said below
- tile_cols: int32 [16, 16, 32], P('row', 'blk'), may hold values from 0 to 3, as said below
- counts: int32 [16, 16], P('row', 'blk'), may hold values from 8 to 32, as said below
- sketch: bfloat16 [65536, 512], P(('row', 'blk')), may hold values from -6 to 6
Outputs:
- basis: float32 [65536, 512], P(('row', 'blk'))
- factor: float32 [512, 512], replicated
The draws below stay inside these ranges and needn't reach their ends.
Inputs may be any that keep to these rules, and one draw needn't show every extreme that they name: In each row group and column group, all 32 slots name distinct pairs (tile_rows, tile_cols). `tile_cols`: see tile_rows: the pairs are distinct in every row group and column group. `counts`: some row group and column group uses all 32 slots.
All inputs are finite; a program needn't handle non-finite values.
Results may differ from the reference program's by a relative error of at most 0.0027.
Values may be sent and summed in bfloat16 or wider, within the bound.
A program may use at most 128 MiB of HBM per device.

```python
import math
import jax
import jax.numpy as jnp
from jax import lax

TILE = 256
K = 512
RB = 16
CB = 4
NT = 32
RGROUPS = 16
CGROUPS = 16
ROWS = 65536


def tile_places(key):
    keys = jax.random.split(key, RGROUPS * CGROUPS)
    places = jax.vmap(lambda single: jax.random.permutation(single, RB * CB)[:NT])(keys)
    return places.reshape(RGROUPS, CGROUPS, NT).astype(jnp.int32)


def draw_tile_rows(key, part):
    return tile_places(key) // CB


def draw_tile_cols(key, part):
    return tile_places(key) % CB


def draw_counts(key, part):
    key = jax.random.fold_in(key, 5)
    first, second = jax.random.split(key)
    filled = jax.random.randint(first, (RGROUPS * CGROUPS,), NT // 4, NT + 1)
    chosen = jax.random.randint(second, (), 0, RGROUPS * CGROUPS)
    filled = filled.at[chosen].set(NT)
    return filled.reshape(RGROUPS, CGROUPS).astype(jnp.int32)


def draw_tiles(key, part):
    key = jax.random.fold_in(key, 9)
    shape = (RGROUPS, CGROUPS, NT, TILE, TILE)
    ramp = jnp.arange(RGROUPS, dtype=jnp.float32) / max(RGROUPS - 1, 1)
    amplitude = jnp.exp(0.5 * math.log(3.0) * ramp).reshape(RGROUPS, 1, 1, 1, 1)
    scale = 1.0 / math.sqrt(TILE * NT)
    values = jax.random.normal(key, shape, jnp.float32)
    return (values * amplitude * scale).astype(jnp.bfloat16)


def steps_of(rng, shape, pieces, smallest, high):
    loudness, own = 1.0, jax.random.fold_in(rng, 6)
    for dim, blocks in pieces:
        steps = jnp.exp(jax.random.uniform(jax.random.fold_in(own, dim), (blocks,), jnp.float32, smallest / len(pieces), high / len(pieces)))
        loudness = loudness * jnp.repeat(steps, shape[dim] // blocks).reshape([-1 if axis == dim else 1 for axis in range(len(shape))])
    return loudness


def scatter_about(key, extent, scale, bound, cuts=(), kind=jnp.bfloat16):
    level = steps_of(key, extent, cuts, -0.22, 0.18) if cuts else 1.0
    entries = jax.random.normal(key, extent, jnp.float32) * scale * level
    return jnp.minimum(jnp.maximum(entries, -bound), bound).astype(kind)


def setup_inputs(seed: int = 0) -> dict:
    splits = jax.random.split(jax.random.key(seed), 6)
    return {
        "tiles": draw_tiles(jax.random.fold_in(splits[5], 71), 0),
        "tile_rows": draw_tile_rows(jax.random.fold_in(splits[5], 71), 0),
        "tile_cols": draw_tile_cols(jax.random.fold_in(splits[5], 71), 0),
        "counts": draw_counts(jax.random.fold_in(splits[5], 71), 0),
        "sketch": scatter_about(splits[4], (ROWS, K), 1.0, 6.0, ((0, 256),)),
    }


def reference(tiles, tile_rows, tile_cols, counts, sketch):
    high = lax.Precision.HIGHEST
    live = jnp.arange(NT)[None, None, :] < counts[:, :, None]
    col_hot = ((tile_cols[..., None] == jnp.arange(CB)) & live[..., None]).astype(jnp.float32)
    row_hot = ((tile_rows[..., None] == jnp.arange(RB)) & live[..., None]).astype(jnp.float32)
    sketch_blocks = sketch.reshape(RGROUPS, RB, TILE, K)

    def column_step(carry, group):
        blocks = tiles[group].astype(jnp.float32)
        picked = sketch_blocks[group][tile_rows[group]].astype(jnp.float32)
        products = jnp.einsum('btij,btik->btjk', blocks, picked, precision=high)
        term = jnp.einsum('btc,btjk->bcjk', col_hot[group], products, precision=high)
        return (carry + term, None)
    start = jnp.zeros((CGROUPS, CB, TILE, K), jnp.float32)
    column_sum, unused = lax.scan(column_step, start, jnp.arange(RGROUPS))
    column_image = column_sum.astype(jnp.bfloat16)

    def image_group(group):
        blocks = tiles[group].astype(jnp.float32)
        picked = column_image[jnp.arange(CGROUPS)[:, None], tile_cols[group]].astype(jnp.float32)
        products = jnp.einsum('btij,btjk->btik', blocks, picked, precision=high)
        rows_out = jnp.einsum('btr,btik->rik', row_hot[group], products, precision=high)
        return rows_out.reshape(RB * TILE, K)
    image = lax.map(image_group, jnp.arange(RGROUPS)).reshape(ROWS, K)
    gram = jnp.dot(image.T, image, precision=high) / ROWS
    lower = jnp.linalg.cholesky(gram)
    basis = lax.linalg.triangular_solve(lower, image, left_side=False, lower=True, transpose_a=True)
    return (basis, lower.T)
```

```python
import functools
import jax
import jax.numpy as jnp
from jax import lax
from jax.experimental import pallas as pl
from jax.experimental.pallas import tpu as pltpu
from jax.sharding import PartitionSpec as P

F32 = jnp.float32
BF16 = jnp.bfloat16
MESH = pl.DeviceIdType.MESH
EDGE = 256
RB = 16
CB = 4
K = 512
PX, PY, PZ = 4, 4, 8


def where_am_i():
    row = lax.axis_index("row")
    blk = lax.axis_index("blk")
    return row // 2, row % 2, blk // PX, blk % PX


class Net:
    def __init__(self, send_sems, recv_sems):
        self.send_sems, self.recv_sems = send_sems, recv_sems
        self.used = 0
        self.z, self.c, self.y, self.x = where_am_i()

    def device(self, dz=0, dc=0, dy=0, dx=0):
        z = lax.rem(self.z + dz + PZ, PZ)
        c = 1 - self.c if dc else self.c
        y = lax.rem(self.y + dy + PY, PY)
        x = lax.rem(self.x + dx + PX, PX)
        return {"row": z * 2 + c, "blk": y * PX + x}

    def greet(self, steps):
        barrier = pltpu.get_barrier_semaphore()
        for step in steps:
            pl.semaphore_signal(barrier, inc=1, device_id=self.device(**step), device_id_type=MESH)
        pl.semaphore_wait(barrier, len(steps))

    def copy(self, src, dst, **step):
        slot = self.used
        self.used += 1
        return pltpu.make_async_remote_copy(
            src_ref=src, dst_ref=dst, send_sem=self.send_sems.at[slot], recv_sem=self.recv_sems.at[slot],
            device_id=self.device(**step), device_id_type=MESH)


NEIGHBOURS = [dict(dx=1), dict(dx=-1), dict(dy=1), dict(dy=-1), dict(dz=1), dict(dz=-1), dict(dc=1)]


def build_dense(slot_ref, tiles, dense):
    @pl.loop(0, RB)
    def _(i):
        for c in range(CB):
            slot = slot_ref[i * CB + c]
            keep = jnp.where(slot >= 0, 1.0, 0.0).astype(BF16)
            dense[i, :, c * EDGE:(c + 1) * EDGE] = tiles[jnp.maximum(slot, 0)] * keep


def column_kernel(slot_ref, tiles_hbm, sketch_ref, out, tiles, dense, gath, part, pair, chain, dma_sem, send_sems, recv_sems):
    net = Net(send_sems, recv_sems)
    load = pltpu.make_async_copy(tiles_hbm, tiles, dma_sem)
    load.start()
    mine = net.y * PX + net.x
    flipped = sketch_ref[...].astype(F32).T.astype(BF16)
    gath[mine] = flipped
    net.greet(NEIGHBOURS)
    started = []

    def start(copy):
        copy.start()
        started.append(copy)
        return copy

    half = EDGE
    axes = [("dx", "dy"), ("dy", "dx")]
    arrive = {}

    def slot_of(h, dp, dq):
        dx, dy = (dp, dq) if h == 0 else (dq, dp)
        return lax.rem(net.y + dy + PY, PY) * PX + lax.rem(net.x + dx + PX, PX)

    def push(h, dp, dq, axis, sign, key):
        where = gath.at[slot_of(h, dp, dq), pl.ds(h * half, half), :]
        arrive[key] = start(net.copy(where, where, **{axis: sign}))

    def received(h, dp, dq, key):
        where = gath.at[slot_of(h, dp, dq), pl.ds(h * half, half), :]
        slot = arrive[key]
        pltpu.make_async_remote_copy(
            src_ref=where, dst_ref=where, send_sem=slot_sem(key)[0], recv_sem=slot_sem(key)[1],
            device_id=net.device(dx=1), device_id_type=MESH).wait_recv()

    numbers = {}

    def slot_sem(key):
        return send_sems.at[numbers[key]], recv_sems.at[numbers[key]]

    def go(h, dp, dq, axis, sign, key):
        numbers[key] = net.used
        push(h, dp, dq, axis, sign, key)

    def multiply(h, dp, dq):
        block = gath[slot_of(h, dp, dq), h * half:(h + 1) * half, :]
        i = slot_of(h, dp, dq)
        for c in range(CB):
            prod = jnp.dot(block, dense[i, :, c * EDGE:(c + 1) * EDGE], preferred_element_type=F32)
            for s in range(2):
                rows = slice(h * half, (h + 1) * half)
                part[2 * c + s, rows, :] += prod[:, s * 128:(s + 1) * 128]

    for h in range(2):
        p, q = axes[h]
        go(h, 0, 0, p, 1, (h, -1, 0))
        go(h, 0, 0, p, -1, (h, 1, 0))
    for h in range(2):
        p, q = axes[h]
        go(h, 0, 0, q, 1, (h, 0, -1))
        go(h, 0, 0, q, -1, (h, 0, 1))
    load.wait()
    build_dense(slot_ref, tiles, dense)
    part[...] = jnp.zeros_like(part)
    for h in range(2):
        multiply(h, 0, 0)
    order = [(-1, 0), (1, 0), (0, -1), (0, 1), (2, 0), (-1, -1), (-1, 1), (0, 2), (1, -1), (1, 1), (-1, 2), (2, -1), (2, 1), (1, 2), (2, 2)]
    for dp, dq in order:
        for h in range(2):
            p, q = axes[h]
            received(h, dp, dq, (h, dp, dq))
            if dq == 0:
                if dp == -1:
                    go(h, dp, 0, p, 1, (h, 2, 0))
                go(h, dp, 0, q, 1, (h, dp, -1))
                go(h, dp, 0, q, -1, (h, dp, 1))
            elif dq == -1 and dp in (0, 2):
                go(h, dp, dq, q, 1, (h, dp, 2))
            elif dq == 1 and dp in (-1, 1):
                go(h, dp, dq, q, -1, (h, dp, 2))
        for h in range(2):
            multiply(h, dp, dq)

    own = pl.multiple_of(net.c * half, half)
    other = pl.multiple_of((1 - net.c) * half, half)

    def slab(d):
        return lax.rem(net.z + d + PZ, PZ)

    slabs = [4, 3, -3, 2, -2, 1, -1, 0]
    pairs = {}
    for d in slabs:
        pairs[d] = start(net.copy(part.at[slab(d), pl.ds(other, half), :], pair.at[slab(d)], dc=1))
    sub = half // 2

    def rows(u):
        return pl.ds(pl.multiple_of(own + u * sub, sub), sub)

    def merge(d):
        pairs[d].wait_recv()
        part[slab(d), pl.ds(own, half), :] += pair[slab(d)]

    longest = {(0, 1): 4, (0, -1): 3, (1, 1): 3, (1, -1): 4}
    hops = {}

    def hop(u, sign, dist):
        n = len(hops)
        hops[u, sign, dist] = start(net.copy(part.at[slab(sign * dist), rows(u), :], chain.at[n], dz=sign)), n

    def landed(u, sign, dist):
        copy, n = hops[u, sign, dist + 1]
        copy.wait_recv()
        part[slab(sign * dist), rows(u), :] += chain[n]

    merge(4)
    hop(0, 1, 4)
    hop(1, -1, 4)
    merge(3)
    hop(1, 1, 3)
    merge(-3)
    hop(0, -1, 3)
    landed(0, 1, 3)
    hop(0, 1, 3)
    landed(1, -1, 3)
    hop(1, -1, 3)
    merge(2)
    merge(-2)
    for dist in (2, 1):
        for u, sign in ((1, 1), (0, -1), (0, 1), (1, -1)):
            landed(u, sign, dist)
            hop(u, sign, dist)
        if dist == 2:
            merge(1)
            merge(-1)
    merge(0)
    for u, sign in ((1, 1), (0, -1), (0, 1), (1, -1)):
        landed(u, sign, 0)

    def place(u, d, core):
        return out.at[core * 2 + u, pl.ds(pl.multiple_of(slab(d) * 128, 128), 128), :]

    ring = {}

    def send(u, sign, dist):
        where = place(u, -sign * dist, net.c)
        ring[u, sign, dist + 1] = start(net.copy(where, where, dz=sign))

    shared = []

    def share(u, d):
        where = place(u, d, net.c)
        shared.append(start(net.copy(where, where, dc=1)))

    for u in range(2):
        out[net.c * 2 + u, pl.ds(pl.multiple_of(net.z * 128, 128), 128), :] = part[net.z, rows(u), :].T.astype(BF16)
        send(u, 1, 0)
        send(u, -1, 0)
    for u in range(2):
        share(u, 0)
    for dist in range(1, 5):
        for u, sign in ((0, 1), (1, -1), (1, 1), (0, -1)):
            if dist > longest[u, sign]:
                continue
            ring[u, sign, dist].wait_recv()
            if dist < longest[u, sign]:
                send(u, sign, dist)
            share(u, -sign * dist)
    for copy in shared:
        copy.wait_recv()
    for copy in started:
        copy.wait_send()


def column_image(slots, tiles, sketch):
    return pl.pallas_call(
        column_kernel,
        name="column_image",
        out_shape=jax.ShapeDtypeStruct((4, 1024, 128), BF16),
        in_specs=[pl.BlockSpec(memory_space=pltpu.SMEM), pl.BlockSpec(memory_space=pl.ANY), pl.BlockSpec(memory_space=pltpu.VMEM)],
        out_specs=pl.BlockSpec(memory_space=pltpu.VMEM),
        scratch_shapes=[
            pltpu.VMEM((32, EDGE, EDGE), BF16),
            pltpu.VMEM((RB, EDGE, CB * EDGE), BF16),
            pltpu.VMEM((RB, K, EDGE), BF16),
            pltpu.VMEM((8, K, 128), F32),
            pltpu.VMEM((8, EDGE, 128), F32),
            pltpu.VMEM((14, 128, 128), F32),
            pltpu.SemaphoreType.DMA,
            pltpu.SemaphoreType.DMA((100,)),
            pltpu.SemaphoreType.DMA((100,)),
        ],
        compiler_params=pltpu.CompilerParams(collective_id=0, has_side_effects=True, vmem_limit_bytes=56 << 20),
    )(slots, tiles, sketch)


def slot_table(tile_rows, tile_cols, counts):
    slots = jnp.arange(tile_rows.shape[0], dtype=jnp.int32)
    spot = tile_rows * CB + tile_cols
    hit = (spot[None, :] == jnp.arange(RB * CB)[:, None]) & (slots < counts)[None, :]
    return jnp.max(jnp.where(hit, slots[None, :], -1), axis=1)


HIGH = lax.Precision.HIGHEST


def reach():
    steps = [dict(dc=1)]
    steps += [dict(dx=d) for d in (1, -1, 2)]
    steps += [dict(dy=d) for d in (1, -1, 2)]
    steps += [dict(dz=d) for d in (1, -1, 2, -2, 3, -3, 4)]
    return steps


PANELS = [(i, j) for j in range(4) for i in range(j + 1)]
GROWS = 1280


def image_kernel(slot_ref, tiles_hbm, ci, image, gram, tiles, dense, acc, far, sum2, in1, in2, gbuf, gx, gy, gz, gpair, dma_sem, send_sems, recv_sems):
    net = Net(send_sems, recv_sems)
    load = pltpu.make_async_copy(tiles_hbm, tiles, dma_sem)
    load.start()
    net.greet(reach())
    load.wait()
    build_dense(slot_ref, tiles, dense)
    started = []

    def start(copy):
        copy.start()
        started.append(copy)
        return copy

    def begin(copy):
        copy.start()
        return copy

    axes = [("dx", "dy"), ("dy", "dx")]

    def block_of(h, dp, dq):
        dx, dy = (dp, dq) if h == 0 else (dq, dp)
        return lax.rem(net.y + dy + PY, PY) * PX + lax.rem(net.x + dx + PX, PX)

    def product(h, dp, dq):
        left = dense[block_of(h, dp, dq)]
        right = jnp.concatenate([ci[2 * h], ci[2 * h + 1]], axis=1)
        return jnp.dot(left, right, preferred_element_type=F32)

    QS = (2, 1, -1, 0)
    moves = {}

    def send1(h, dp, dq, sign):
        n = len(moves)
        moves[h, dp, dq] = start(net.copy(far.at[n], in1.at[n], **{axes[h][0]: sign})), n

    def via(dq):
        return 1 if dq in (0, 2) else -1

    def fill(h, dp, dq, value):
        far[len(moves)] = value.astype(BF16)

    for dq in QS:
        for h in range(2):
            fill(h, 2, dq, product(h, 2, dq))
            send1(h, 2, dq, via(dq))
    for dq in QS:
        for h in range(2):
            s = -via(dq)
            fill(h, s, dq, product(h, s, dq))
            send1(h, s, dq, s)
    for dq in QS:
        for h in range(2):
            s = via(dq)
            value = product(h, s, dq)
            copy, n = moves[h, 2, dq]
            copy.wait_recv()
            fill(h, s, dq, value + in1[n].astype(F32))
            send1(h, s, dq, s)
    moves2 = {}
    rows_half = EDGE // 2

    def send2(h, dq, piece, sign):
        n = len(moves2)
        part = pl.ds(piece * rows_half, rows_half)
        moves2[h, dq, piece] = start(net.copy(sum2.at[h, dq % 4, part, :], in2.at[n], **{axes[h][1]: sign})), n

    for dq in QS:
        for h in range(2):
            value = product(h, 0, dq)
            for s in (-via(dq), via(dq)):
                copy, n = moves[h, s, dq]
                copy.wait_recv()
                value = value + in1[n].astype(F32)
            sum2[h, dq % 4] = value
            if dq == 2:
                send2(h, 2, 0, 1)
                send2(h, 2, 1, -1)
            elif dq != 0:
                near = 0 if dq == -1 else 1
                send2(h, dq, near, dq)
    for dq in (1, -1):
        for h in range(2):
            through = 0 if dq == 1 else 1
            copy, n = moves2[h, 2, through]
            copy.wait_recv()
            sum2[h, dq % 4, through * rows_half:(through + 1) * rows_half, :] += in2[n]
            send2(h, dq, through, dq)
    for h in range(2):
        for piece in range(2):
            value = sum2[h, 0, piece * rows_half:(piece + 1) * rows_half, :]
            for dq in (1, -1):
                copy, n = moves2[h, dq, piece]
                copy.wait_recv()
                value = value + in2[n]
            image[piece * rows_half:(piece + 1) * rows_half, h * EDGE:(h + 1) * EDGE] = value

    scale = 1.0 / (lax.axis_size("row") * lax.axis_size("blk") * EDGE)
    for n, (i, j) in enumerate(PANELS):
        gbuf[n * 128:(n + 1) * 128, :] = lax.dot_general(
            image[:, i * 128:(i + 1) * 128], image[:, j * 128:(j + 1) * 128], (((0,), (0,)), ((), ())),
            precision=HIGH, preferred_element_type=F32) * scale
    base = pl.multiple_of(net.c * 640, 8)
    pair = start(net.copy(gbuf.at[pl.ds(pl.multiple_of((1 - net.c) * 640, 8), 640), :], gpair, dc=1))
    pair.wait_recv()
    gbuf[pl.ds(base, 640), :] += gpair[...]

    def quarter(at, pos, d, size):
        return pl.ds(pl.multiple_of(at + lax.rem(pos + d + 4, 4) * size, 8), size)

    def spread(axis, pos, at, size, land):
        copies = [begin(net.copy(gbuf.at[quarter(at, pos, d, size), :], land.at[n], **{axis: d})) for n, d in enumerate((2, 1, -1))]
        value = gbuf[quarter(at, pos, 0, size), :]
        for n, copy in enumerate(copies):
            copy.wait_recv()
            value = value + land[n]
        for copy in copies:
            copy.wait_send()
        gbuf[quarter(at, pos, 0, size), :] = value
        return pl.multiple_of(at + pos * size, 8)

    base_x = spread("dx", net.x, base, 160, gx)
    base_y = spread("dy", net.y, base_x, 40, gy)
    copies = [begin(net.copy(gbuf.at[pl.ds(base_y, 40), :], gz.at[n], dz=d)) for n, d in enumerate((4, 3, -3, 2, -2, 1, -1))]
    for copy in copies:
        copy.wait_recv()
    for copy in copies:
        copy.wait_send()
    value = None
    gz[7] = gbuf[pl.ds(base_y, 40), :]
    offsets = (4, 3, -3, 2, -2, 1, -1, 0)
    for place in range(PZ):
        d = lax.rem(net.z - place + PZ, PZ)
        at = 0
        for n, o in enumerate(offsets):
            at = at + jnp.where(d == o % PZ, n, 0)
        term = gz[at]
        value = term if value is None else value + term
    gram[pl.ds(base_y, 40), :] = value

    def collect(axis, at, size):
        where = gram.at[pl.ds(at, size), :]
        copies = [start(net.copy(where, where, **{axis: d})) for d in ((2, 1, -1) if axis != "dc" else (1,))]
        for copy in copies:
            copy.wait_recv()

    collect("dy", base_y, 40)
    collect("dx", base_x, 160)
    collect("dc", base, 640)
    for copy in started:
        copy.wait_send()


def image_and_gram(slots, tiles, ci):
    vmem = pl.BlockSpec(memory_space=pltpu.VMEM)
    return pl.pallas_call(
        image_kernel,
        name="image_and_gram",
        out_shape=[jax.ShapeDtypeStruct((EDGE, K), F32), jax.ShapeDtypeStruct((GROWS, 128), F32)],
        in_specs=[pl.BlockSpec(memory_space=pltpu.SMEM), pl.BlockSpec(memory_space=pl.ANY), vmem],
        out_specs=[vmem, vmem],
        scratch_shapes=[
            pltpu.VMEM((32, EDGE, EDGE), BF16),
            pltpu.VMEM((RB, EDGE, CB * EDGE), BF16),
            pltpu.VMEM((8, 128), F32),
            pltpu.VMEM((24, EDGE, EDGE), BF16),
            pltpu.VMEM((2, 4, EDGE, EDGE), F32),
            pltpu.VMEM((24, EDGE, EDGE), BF16),
            pltpu.VMEM((12, EDGE // 2, EDGE), F32),
            pltpu.VMEM((GROWS, 128), F32),
            pltpu.VMEM((3, 160, 128), F32),
            pltpu.VMEM((3, 40, 128), F32),
            pltpu.VMEM((8, 40, 128), F32),
            pltpu.VMEM((640, 128), F32),
            pltpu.SemaphoreType.DMA,
            pltpu.SemaphoreType.DMA((64,)),
            pltpu.SemaphoreType.DMA((64,)),
        ],
        compiler_params=pltpu.CompilerParams(collective_id=1, has_side_effects=True, vmem_limit_bytes=56 << 20),
    )(slots, tiles, ci)


def lane(x, j):
    return jnp.take_along_axis(x, jnp.full(x.shape, j, jnp.int32), axis=1)


def sub(x, i):
    return jnp.broadcast_to(x[i:i + 1, :], x.shape)


def factor_block(S, E):
    rid = lax.broadcasted_iota(jnp.int32, (8, 128), 0)
    lid = lax.broadcasted_iota(jnp.int32, (8, 128), 1)
    E = [(lid == rid + 8 * i).astype(F32) for i in range(16)]
    S = list(S)
    for g in range(16):
        cols = [lane(S[g], 8 * g + k) for k in range(8)]
        a = {(i, k): sub(cols[k], i) for k in range(8) for i in range(k, 8)}
        r, l, m = [None] * 8, {}, {}
        for k in range(8):
            r[k] = lax.rsqrt(a[k, k])
            for i in range(k + 1, 8):
                l[i, k] = a[i, k] * r[k]
            for i in range(k + 1, 8):
                for n in range(k + 1, i + 1):
                    a[i, n] = a[i, n] - l[i, k] * l[n, k]
        for j in range(8):
            m[j, j] = r[j]
            for i in range(j + 1, 8):
                t = l[i, j] * m[j, j]
                for k in range(j + 1, i):
                    t = t + l[i, k] * m[k, j]
                m[i, j] = -(t * r[i])
        u = e = None
        for k in range(8):
            c = jnp.zeros((8, 128), F32)
            for i in range(k, 8):
                c = jnp.where(rid == i, m[i, k], c)
            tu, te = c * sub(S[g], k), c * sub(E[g], k)
            u, e = (tu, te) if u is None else (u + tu, e + te)
        S[g], E[g] = u, e
        if g < 15:
            us, es = [sub(u, k) for k in range(8)], [sub(e, k) for k in range(8)]
            turned = u.T
            for i in range(g + 1, 16):
                c = turned[8 * i:8 * i + 8, :]
                for k in range(8):
                    ck = jnp.broadcast_to(c[:, k:k + 1], (8, 128))
                    S[i] = S[i] - ck * us[k]
                    E[i] = E[i] - ck * es[k]
    S = [jnp.where(lid >= rid + 8 * i, s, 0.0) for i, s in enumerate(S)]
    return S, E


def dot(a, b, dims=((1,), (0,))):
    return lax.dot_general(a, b, (dims, ((), ())), precision=HIGH, preferred_element_type=F32)


def basis_kernel(gram, image, basis, factor, S, inv):
    def panel(i, j):
        return slice(j * 128, (j + 1) * 128), slice(i * 128, (i + 1) * 128)

    index = {p: n for n, p in enumerate(PANELS)}
    for (i, j), n in index.items():
        S[n] = gram[n * 128:(n + 1) * 128, :]
    span = lambda b: slice(b * 128, (b + 1) * 128)
    for b in range(4):
        for i in range(b):
            factor[span(b), span(i)] = jnp.zeros((128, 128), F32)

    for b in range(4):
        d = index[b, b]
        if b:
            for k in range(b):
                u = factor[span(k), span(b)]
                for j in range(b, 4):
                    pass
        rows = [S[d, 8 * g:8 * g + 8, :] for g in range(16)]
        rows, e = factor_block(rows, None)
        for g in range(16):
            factor[b * 128 + 8 * g:b * 128 + 8 * g + 8, span(b)] = rows[g]
            inv[8 * g:8 * g + 8, :] = e[g]
        for j in range(b + 1, 4):
            factor[span(b), span(j)] = dot(inv[...], S[index[b, j]])
        for i in range(b + 1, 4):
            for j in range(i, 4):
                S[index[i, j]] -= dot(factor[span(b), span(i)], factor[span(b), span(j)], ((0,), (0,)))
        value = image[:, span(b)]
        for k in range(b):
            value = value - dot(basis[:, span(k)], factor[span(k), span(b)])
        basis[:, span(b)] = dot(value, inv[...], ((1,), (1,)))


def orthonormalize(gram, image):
    vmem = pl.BlockSpec(memory_space=pltpu.VMEM)
    return pl.pallas_call(
        basis_kernel,
        name="orthonormalize",
        out_shape=[jax.ShapeDtypeStruct((EDGE, K), F32), jax.ShapeDtypeStruct((K, K), F32)],
        in_specs=[vmem, vmem],
        out_specs=[vmem, vmem],
        scratch_shapes=[pltpu.VMEM((10, 128, 128), F32), pltpu.VMEM((128, 128), F32)],
        compiler_params=pltpu.CompilerParams(vmem_limit_bytes=32 << 20),
    )(gram, image)


def local(tiles, tile_rows, tile_cols, counts, sketch):
    blocks = tiles[0, 0]
    slots = slot_table(tile_rows[0, 0], tile_cols[0, 0], counts[0, 0])
    ci = column_image(slots, blocks, sketch)
    image, gram = image_and_gram(slots, blocks, ci)
    return orthonormalize(gram, image)


def solution(mesh):
    in_specs = (
        P("row", "blk", None, None, None),
        P("row", "blk", None),
        P("row", "blk", None),
        P("row", "blk"),
        P(("row", "blk"), None),
    )
    out_specs = (P(("row", "blk"), None), P())
    return jax.shard_map(local, mesh=mesh, in_specs=in_specs, out_specs=out_specs, check_vma=False)
```

```python
import functools
import jax
import jax.numpy as jnp
from jax import lax
from jax.experimental import pallas as pl
from jax.experimental.pallas import tpu as pltpu
from jax.sharding import PartitionSpec as P

F32 = jnp.float32
BF16 = jnp.bfloat16
MESH = pl.DeviceIdType.MESH
EDGE = 256
RB = 16
CB = 4
K = 512
PX, PY, PZ = 4, 4, 8


def where_am_i():
    row = lax.axis_index("row")
    blk = lax.axis_index("blk")
    return row // 2, row % 2, blk // PX, blk % PX


class Net:
    def __init__(self, send_sems, recv_sems):
        self.send_sems, self.recv_sems = send_sems, recv_sems
        self.used = 0
        self.z, self.c, self.y, self.x = where_am_i()

    def device(self, dz=0, dc=0, dy=0, dx=0):
        z = lax.rem(self.z + dz + PZ, PZ)
        c = 1 - self.c if dc else self.c
        y = lax.rem(self.y + dy + PY, PY)
        x = lax.rem(self.x + dx + PX, PX)
        return {"row": z * 2 + c, "blk": y * PX + x}

    def greet(self, steps):
        barrier = pltpu.get_barrier_semaphore()
        for step in steps:
            pl.semaphore_signal(barrier, inc=1, device_id=self.device(**step), device_id_type=MESH)
        pl.semaphore_wait(barrier, len(steps))

    def copy(self, src, dst, **step):
        slot = self.used
        self.used += 1
        return pltpu.make_async_remote_copy(
            src_ref=src, dst_ref=dst, send_sem=self.send_sems.at[slot], recv_sem=self.recv_sems.at[slot],
            device_id=self.device(**step), device_id_type=MESH)


NEIGHBOURS = [dict(dx=1), dict(dx=-1), dict(dy=1), dict(dy=-1), dict(dz=1), dict(dz=-1), dict(dc=1)]


def build_dense(slot_ref, tiles, dense):
    @pl.loop(0, RB)
    def _(i):
        for c in range(CB):
            slot = slot_ref[i * CB + c]
            keep = jnp.where(slot >= 0, 1.0, 0.0).astype(BF16)
            dense[i, :, c * EDGE:(c + 1) * EDGE] = tiles[jnp.maximum(slot, 0)] * keep


def slot_table(tile_rows, tile_cols, counts):
    slots = jnp.arange(tile_rows.shape[0], dtype=jnp.int32)
    spot = tile_rows * CB + tile_cols
    hit = (spot[None, :] == jnp.arange(RB * CB)[:, None]) & (slots < counts)[None, :]
    return jnp.max(jnp.where(hit, slots[None, :], -1), axis=1)


HIGH = lax.Precision.HIGHEST


def reach():
    steps = [dict(dc=1)]
    steps += [dict(dx=d) for d in (1, -1, 2)]
    steps += [dict(dy=d) for d in (1, -1, 2)]
    steps += [dict(dz=d) for d in (1, -1, 2, -2, 3, -3, 4)]
    return steps


PANELS = [(i, j) for j in range(4) for i in range(j + 1)]

GR = (512, 1024)


def lane(x, j):
    return jnp.take_along_axis(x, jnp.full(x.shape, j, jnp.int32), axis=1)


def sub(x, i):
    return jnp.broadcast_to(x[i:i + 1, :], x.shape)


def factor_block(S, E):
    rid = lax.broadcasted_iota(jnp.int32, (8, 128), 0)
    lid = lax.broadcasted_iota(jnp.int32, (8, 128), 1)
    E[:] = [(lid == rid + 8 * i).astype(F32) for i in range(16)]
    for g in range(16):
        cols = [lane(S[g], 8 * g + k) for k in range(8)]
        a = {(i, k): sub(cols[k], i) for k in range(8) for i in range(k, 8)}
        r, l, m = [None] * 8, {}, {}
        for k in range(8):
            r[k] = lax.rsqrt(a[k, k])
            for i in range(k + 1, 8):
                l[i, k] = a[i, k] * r[k]
            for i in range(k + 1, 8):
                for n in range(k + 1, i + 1):
                    a[i, n] = a[i, n] - l[i, k] * l[n, k]
        for j in range(8):
            m[j, j] = r[j]
            for i in range(j + 1, 8):
                t = l[i, j] * m[j, j]
                for k in range(j + 1, i):
                    t = t + l[i, k] * m[k, j]
                m[i, j] = -(t * r[i])
        u = e = None
        for k in range(8):
            c = jnp.zeros((8, 128), F32)
            for i in range(k, 8):
                c = jnp.where(rid == i, m[i, k], c)
            tu, te = c * sub(S[g], k), c * sub(E[g], k)
            u, e = (tu, te) if u is None else (u + tu, e + te)
        S[g], E[g] = u, e
        if g < 15:
            us, es = [sub(u, k) for k in range(8)], [sub(e, k) for k in range(8)]
            turned = u.T
            for i in range(g + 1, 16):
                c = turned[8 * i:8 * i + 8, :]
                for k in range(8):
                    ck = jnp.broadcast_to(c[:, k:k + 1], (8, 128))
                    S[i] = S[i] - ck * us[k]
                    E[i] = E[i] - ck * es[k]
            yield CHOL
    S[:] = [jnp.where(lid >= rid + 8 * i, s, 0.0) for i, s in enumerate(S)]


def dot(a, b, dims=((1,), (0,))):
    return lax.dot_general(a, b, (dims, ((), ())), precision=HIGH, preferred_element_type=F32)


def weave(*works):
    queue = [[begin, n, work] for n, (begin, work) in enumerate(works)]
    while queue:
        entry = min(queue)
        try:
            entry[0] += next(entry[2])
        except StopIteration:
            queue.remove(entry)


def power_kernel(slot_ref, tiles_hbm, sketch_ref, basis, factor, image, gram0, gram1, S, inv, tiles, dense, gath, part, pair, chain, ci, acc, far, in1, sum2, in2,
                 gbuf0, gbuf1, gpair, g1, g2, gstage, gz, dma_sem, send_sems, recv_sems):
    net = Net(send_sems, recv_sems)
    load = pltpu.make_async_copy(tiles_hbm, tiles, dma_sem)
    load.start()
    mine = net.y * PX + net.x
    gath[mine] = sketch_ref[...].astype(F32).T.astype(BF16)
    net.greet(reach())
    started = []
    axes = [("dx", "dy"), ("dy", "dx")]

    def start(copy):
        copy.start()
        started.append(copy)
        return copy

    def begin(copy):
        copy.start()
        return copy

    def block_of(h, dp, dq):
        dx, dy = (dp, dq) if h == 0 else (dq, dp)
        return lax.rem(net.y + dy + PY, PY) * PX + lax.rem(net.x + dx + PX, PX)

    def slab(d):
        return lax.rem(net.z + d + PZ, PZ)

    def gather(t):
        base = 256 * t
        arrive = {}
        got = set()

        def go(h, dp, dq, axis, sign, key):
            where = gath.at[block_of(h, dp, dq), pl.ds(base + h * 128, 128), :]
            arrive[key] = net.used
            start(net.copy(where, where, **{axis: sign}))

        def received(h, dp, dq):
            where = gath.at[block_of(h, dp, dq), pl.ds(base + h * 128, 128), :]
            n = arrive[h, dp, dq]
            pltpu.make_async_remote_copy(
                src_ref=where, dst_ref=where, send_sem=send_sems.at[n], recv_sem=recv_sems.at[n],
                device_id=net.device(dx=1), device_id_type=MESH).wait_recv()

        def multiply(dx, dy):
            i = block_of(0, dx, dy)
            block = gath[i, base:base + 256, :]
            for c in range(CB):
                prod = jnp.dot(block, dense[i, :, c * EDGE:(c + 1) * EDGE], preferred_element_type=F32)
                for s in range(2):
                    piece = prod[:, s * 128:(s + 1) * 128]
                    if (dx, dy) == (0, 0):
                        part[2 * c + s, base:base + 256, :] = piece
                    else:
                        part[2 * c + s, base:base + 256, :] += piece

        for h in range(2):
            p, q = axes[h]
            go(h, 0, 0, p, 1, (h, -1, 0))
            go(h, 0, 0, p, -1, (h, 1, 0))
        for h in range(2):
            p, q = axes[h]
            go(h, 0, 0, q, 1, (h, 0, -1))
            go(h, 0, 0, q, -1, (h, 0, 1))
        if t == 0:
            load.wait()
            build_dense(slot_ref, tiles, dense)
        yield GATHER[t][0]
        multiply(0, 0)
        order = [(-1, 0), (1, 0), (0, -1), (0, 1), (2, 0), (-1, -1), (-1, 1), (0, 2), (1, -1), (1, 1), (-1, 2), (2, -1), (2, 1), (1, 2), (2, 2)]
        for dp, dq in order:
            for h in range(2):
                p, q = axes[h]
                received(h, dp, dq)
                if dq == 0:
                    if dp == -1:
                        go(h, dp, 0, p, 1, (h, 2, 0))
                    go(h, dp, 0, q, 1, (h, dp, -1))
                    go(h, dp, 0, q, -1, (h, dp, 1))
                elif dq == -1 and dp in (0, 2):
                    go(h, dp, dq, q, 1, (h, dp, 2))
                elif dq == 1 and dp in (-1, 1):
                    go(h, dp, dq, q, -1, (h, dp, 2))
            got.add((dp, dq))
            if (dq, dp) in got:
                for dx, dy in {(dp, dq): 0, (dq, dp): 0}:
                    multiply(dx, dy)
            yield GATHER[t][1]

    def columns(t):
        base = 256 * t
        own = pl.multiple_of(base + net.c * 128, 128)
        other = pl.multiple_of(base + (1 - net.c) * 128, 128)
        pairs, legs, shared = {}, {}, []

        def merge(d):
            pairs[d].wait_recv()
            part[slab(d), pl.ds(own, 128), :] += pair[t, slab(d)]

        def leg(name, d, u, slot, dz):
            src = part.at[slab(d), pl.ds(own, 128) if u is None else pl.ds(pl.multiple_of(own + u * 64, 64), 64), :]
            dst = chain.at[t, slot] if u is None else chain.at[t, slot, pl.ds(0, 64), :]
            legs[name] = start(net.copy(src, dst, dz=dz))

        for d in (4, 3, -3, 1, -1, 2, -2, 0):
            pairs[d] = start(net.copy(part.at[slab(d), pl.ds(other, 128), :], pair.at[t, slab(d)], dc=1))
        yield ZPAIR
        merge(4)
        leg((4, 1), 4, 0, 0, 2)
        leg((4, -1), 4, 1, 1, -2)
        merge(3)
        leg((3, 1), 3, None, 2, 1)
        merge(-3)
        leg((3, -1), -3, None, 3, -1)
        merge(1)
        leg((1, 1), 1, None, 4, 1)
        merge(-1)
        leg((1, -1), -1, None, 5, -1)
        merge(2)
        merge(-2)
        yield ZFAR
        for n, sign in enumerate((1, -1)):
            legs[3, sign].wait_recv()
            part[slab(2 * sign), pl.ds(own, 128), :] += chain[t, 2 + n]
            legs[4, sign].wait_recv()
            part[slab(2 * sign), pl.ds(pl.multiple_of(own + n * 64, 64), 64), :] += chain[t, n, 0:64, :]
            leg((2, sign), 2 * sign, None, 6 + n, 2 * sign)
        merge(0)
        yield ZNEAR
        value = part[net.z, pl.ds(own, 128), :]
        for n, sign in enumerate((1, -1)):
            legs[1, sign].wait_recv()
            value = value + chain[t, 4 + n]
        yield ZLAST
        for n, sign in enumerate((1, -1)):
            legs[2, sign].wait_recv()
            value = value + chain[t, 6 + n]

        def place(d, u=None):
            at = slab(d) * 128 + (0 if u is None else u * 64)
            return ci.at[2 * t + net.c, pl.ds(pl.multiple_of(at, 64), 128 if u is None else 64), :]

        def send(d, dz, u=None):
            return start(net.copy(place(d, u), place(d, u), dz=dz))

        def share(d, u=None):
            shared.append(start(net.copy(place(d, u), place(d, u), dc=1)))

        ci[2 * t + net.c, pl.ds(pl.multiple_of(net.z * 128, 128), 128), :] = value.T.astype(BF16)
        two = {sign: send(0, 2 * sign) for sign in (1, -1)}
        one = {sign: send(0, sign) for sign in (1, -1)}
        share(0)
        yield ZRING
        three, four = {}, {}
        for n, sign in enumerate((1, -1)):
            two[sign].wait_recv()
            four[sign] = send(-2 * sign, 2 * sign, n)
            three[sign] = send(-2 * sign, sign)
            share(-2 * sign)
        for sign in (1, -1):
            one[sign].wait_recv()
            share(-sign)
        yield ZRING
        for sign in (1, -1):
            three[sign].wait_recv()
            share(-3 * sign)
        for n, sign in enumerate((1, -1)):
            four[sign].wait_recv()
            share(4, n)
        yield ZSHARE
        for copy in shared:
            copy.wait_recv()

    def rows_out(t):
        moves, moves2, made = {}, {}, set()
        QS = (2, 1, -1, 0)

        def product(h, dp, dq):
            spot = (dp, dq) if h == 0 else (dq, dp)
            i = block_of(h, dp, dq)
            if spot not in made:
                made.add(spot)
                right = jnp.concatenate([ci[2 * t], ci[2 * t + 1]], axis=1)
                acc[t, i] = jnp.dot(dense[i], right, preferred_element_type=F32)
            return acc[t, i, :, h * 128:(h + 1) * 128]

        def send1(h, dp, dq, sign, value):
            n = len(moves)
            far[t, n] = value.astype(BF16)
            moves[h, dp, dq] = start(net.copy(far.at[t, n], in1.at[t, n], **{axes[h][0]: sign})), n

        def via(dq):
            return 1 if dq in (0, 2) else -1

        def send2(h, dq, piece, sign):
            n = len(moves2)
            moves2[h, dq, piece] = start(net.copy(sum2.at[t, h, dq % 4, pl.ds(piece * 128, 128), :], in2.at[t, n], **{axes[h][1]: sign})), n

        for dq in QS:
            for h in range(2):
                send1(h, 2, dq, via(dq), product(h, 2, dq))
        for dq in QS:
            for h in range(2):
                s = -via(dq)
                send1(h, s, dq, s, product(h, s, dq))
        for dq in QS:
            for h in range(2):
                product(h, via(dq), dq)
                product(h, 0, dq)
            yield RS1[QS.index(dq)]
            for h in range(2):
                s = via(dq)
                copy, n = moves[h, 2, dq]
                copy.wait_recv()
                send1(h, s, dq, s, product(h, s, dq) + in1[t, n].astype(F32))
        for dq in QS:
            yield RS2[QS.index(dq)]
            for h in range(2):
                value = product(h, 0, dq)
                for s in (-via(dq), via(dq)):
                    copy, n = moves[h, s, dq]
                    copy.wait_recv()
                    value = value + in1[t, n].astype(F32)
                sum2[t, h, dq % 4] = value
                if dq == 2:
                    send2(h, 2, 0, 1)
                    send2(h, 2, 1, -1)
                elif dq != 0:
                    send2(h, dq, 0 if dq == -1 else 1, dq)
        for dq in (1, -1):
            yield RS3[dq == -1]
            for h in range(2):
                through = 0 if dq == 1 else 1
                copy, n = moves2[h, 2, through]
                copy.wait_recv()
                sum2[t, h, dq % 4, through * 128:(through + 1) * 128, :] += in2[t, n]
                send2(h, dq, through, dq)
        yield RS4
        for h in range(2):
            for piece in range(2):
                value = sum2[t, h, 0, piece * 128:(piece + 1) * 128, :]
                for dq in (1, -1):
                    copy, n = moves2[h, dq, piece]
                    copy.wait_recv()
                    value = value + in2[t, n]
                image[piece * 128:(piece + 1) * 128, t * 256 + h * 128:t * 256 + (h + 1) * 128] = value

    def moments(t):
        size = GR[t]
        gbuf, out = (gbuf0, gram0) if t == 0 else (gbuf1, gram1)
        scale = 1.0 / (lax.axis_size("row") * lax.axis_size("blk") * EDGE)
        panels = [p for p in PANELS if p[1] // 2 == t]
        for n, (i, j) in enumerate(panels):
            gbuf[n * 128:(n + 1) * 128, :] = lax.dot_general(
                image[:, i * 128:(i + 1) * 128], image[:, j * 128:(j + 1) * 128], (((0,), (0,)), ((), ())),
                precision=HIGH, preferred_element_type=F32) * scale
        gbuf[size - 128:, :] = jnp.zeros((128, 128), F32)
        half, quarter, first, second = size // 2, size // 4, size // 16, size // 64
        base = pl.multiple_of(net.c * half, 256)
        twin = start(net.copy(gbuf.at[pl.ds(pl.multiple_of((1 - net.c) * half, 256), half), :], gpair.at[pl.ds(t * 256, half), :], dc=1))
        yield GM1
        twin.wait_recv()
        gbuf[pl.ds(base, half), :] += gpair[t * 256:t * 256 + half, :]

        def cut(at, pos, d, step):
            return pl.ds(pl.multiple_of(at + lax.rem(pos + d + 4, 4) * step, 8), step)

        place = (net.x, net.y)
        ats = [base + v * quarter for v in range(2)]
        for level, step in enumerate((first, second)):
            copies = {}
            for d in (2, 1, -1):
                for v in range(2):
                    n = {2: 0, 1: 1, -1: 2}[d]
                    land = g1.at[t, v, n, pl.ds(0, step), :] if level == 0 else g2.at[t, v, n, pl.ds(0, step), :]
                    axis = axes[v][level]
                    copies[v, n] = start(net.copy(gbuf.at[cut(ats[v], place[(v + level) % 2], d, step), :], land, **{axis: d}))
            yield GM2
            for v in range(2):
                here = cut(ats[v], place[(v + level) % 2], 0, step)
                value = gbuf[here, :]
                for n in range(3):
                    copies[v, n].wait_recv()
                    value = value + (g1 if level == 0 else g2)[t, v, n, 0:step, :]
                if level == 0:
                    gbuf[here, :] = value
                else:
                    gstage[t, v * second:(v + 1) * second, :] = value
                ats[v] = pl.multiple_of(ats[v] + place[(v + level) % 2] * step, 8)
        both = 2 * second
        offsets = (4, 3, -3, 2, -2, 1, -1, 0)
        copies = [start(net.copy(gstage.at[t, pl.ds(0, both), :], gz.at[t, n, pl.ds(0, both), :], dz=d)) for n, d in enumerate(offsets[:-1])]
        gz[t, 7, 0:both, :] = gstage[t, 0:both, :]
        yield GM3
        for copy in copies:
            copy.wait_recv()
        value = None
        for spot in range(PZ):
            d = lax.rem(net.z - spot + PZ, PZ)
            at = 0
            for n, o in enumerate(offsets):
                at = at + jnp.where(d == o % PZ, n, 0)
            term = gz[t, at, 0:both, :]
            value = term if value is None else value + term
        for v in range(2):
            out[pl.ds(ats[v], second), :] = value[v * second:(v + 1) * second, :]
        for level, step in ((1, second), (0, first)):
            copies = []
            for v in range(2):
                if level == 0:
                    ats[v] = base + v * quarter + place[v % 2] * first
                where = out.at[pl.ds(pl.multiple_of(ats[v], 8), step), :]
                for d in (2, 1, -1):
                    copies.append(start(net.copy(where, where, **{axes[v][level]: d})))
            yield GM2
            for copy in copies:
                copy.wait_recv()
        where = out.at[pl.ds(base, half), :]
        twin = start(net.copy(where, where, dc=1))
        yield GM1
        twin.wait_recv()

    index = {p: n for n, p in enumerate(PANELS)}

    def span(b):
        return slice(b * 128, (b + 1) * 128)

    def panel(i, j):
        n = index[i, j]
        return gram0[span(n), :] if n < 3 else gram1[span(n - 3), :]

    def reduced(i, j, upto):
        value = panel(i, j)
        for k in range(upto):
            value = value - dot(factor[span(k), span(i)], factor[span(k), span(j)], ((0,), (0,)))
        return value

    def solve(b):
        for i in range(b):
            factor[span(b), span(i)] = jnp.zeros((128, 128), F32)
        if b == 2:
            for j in (2, 3):
                for i in (0, 1):
                    factor[span(i), span(j)] = dot(inv[i], reduced(i, j, i))
        yield CHOL
        S[...] = reduced(b, b, b)
        value = image[:, span(b)]
        for k in range(b):
            value = value - dot(basis[:, span(k)], factor[span(k), span(b)])
        yield CHOL
        rows, e = [S[8 * g:8 * g + 8, :] for g in range(16)], []
        yield from factor_block(rows, e)
        for g in range(16):
            factor[b * 128 + 8 * g:b * 128 + 8 * g + 8, span(b)] = rows[g]
            inv[b, 8 * g:8 * g + 8, :] = e[g]
        yield CHOL
        if b % 2 == 0:
            factor[span(b), span(b + 1)] = dot(inv[b], reduced(b, b + 1, b))
        yield CHOL
        basis[:, span(b)] = dot(value, inv[b], ((1,), (1,)))

    def process(t):
        yield from gather(t)
        yield from columns(t)
        yield from rows_out(t)
        yield from moments(t)

        if t == 0:
            yield from solve(0)
            yield from solve(1)

    weave((0.0, process(0)), (SECOND, process(1)))
    weave((0.0, solve(2)))
    weave((0.0, solve(3)))
    for copy in started:
        copy.wait_send()


SECOND = 15.0
GATHER = ((8.0, 1.0), (5.0, 1.2))
ZPAIR, ZFAR, ZNEAR, ZLAST, ZRING, ZSHARE = 3.0, 4.5, 1.0, 3.0, 3.5, 1.5
RS1, RS2, RS3, RS4 = (4.0, 1.2, 1.2, 1.2), (2.5, 1.2, 1.2, 1.2), (1.5, 0.7), 2.5
GM1, GM2, GM3 = 2.0, 3.0, 6.0
CHOL = 0.45


def power_step(slots, tiles, sketch):
    vmem = pl.BlockSpec(memory_space=pltpu.VMEM)
    return pl.pallas_call(
        power_kernel,
        name="power_step",
        out_shape=[jax.ShapeDtypeStruct((EDGE, K), F32), jax.ShapeDtypeStruct((K, K), F32)],
        in_specs=[pl.BlockSpec(memory_space=pltpu.SMEM), pl.BlockSpec(memory_space=pl.ANY), vmem],
        out_specs=[vmem, vmem],
        scratch_shapes=[
            pltpu.VMEM((EDGE, K), F32),
            pltpu.VMEM((GR[0], 128), F32),
            pltpu.VMEM((GR[1], 128), F32),
            pltpu.VMEM((128, 128), F32),
            pltpu.VMEM((4, 128, 128), F32),
            pltpu.VMEM((32, EDGE, EDGE), BF16),
            pltpu.VMEM((RB, EDGE, CB * EDGE), BF16),
            pltpu.VMEM((RB, K, EDGE), BF16),
            pltpu.VMEM((8, K, 128), F32),
            pltpu.VMEM((2, 8, 128, 128), F32),
            pltpu.VMEM((2, 8, 128, 128), F32),
            pltpu.VMEM((4, 1024, 128), BF16),
            pltpu.VMEM((2, RB, EDGE, EDGE), F32),
            pltpu.VMEM((2, 24, EDGE, 128), BF16),
            pltpu.VMEM((2, 24, EDGE, 128), BF16),
            pltpu.VMEM((2, 2, 4, EDGE, 128), F32),
            pltpu.VMEM((2, 12, 128, 128), F32),
            pltpu.VMEM((GR[0], 128), F32),
            pltpu.VMEM((GR[1], 128), F32),
            pltpu.VMEM((768, 128), F32),
            pltpu.VMEM((2, 2, 3, 64, 128), F32),
            pltpu.VMEM((2, 2, 3, 16, 128), F32),
            pltpu.VMEM((2, 32, 128), F32),
            pltpu.VMEM((2, 8, 32, 128), F32),
            pltpu.SemaphoreType.DMA,
            pltpu.SemaphoreType.DMA((320,)),
            pltpu.SemaphoreType.DMA((320,)),
        ],
        compiler_params=pltpu.CompilerParams(collective_id=0, has_side_effects=True, vmem_limit_bytes=60 << 20),
    )(slots, tiles, sketch)


def local(tiles, tile_rows, tile_cols, counts, sketch):
    blocks = tiles[0, 0]
    slots = slot_table(tile_rows[0, 0], tile_cols[0, 0], counts[0, 0])
    basis, factor = power_step(slots, blocks, sketch)
    return basis, factor


def solution(mesh):
    in_specs = (
        P("row", "blk", None, None, None),
        P("row", "blk", None),
        P("row", "blk", None),
        P("row", "blk"),
        P(("row", "blk"), None),
    )
    out_specs = (P(("row", "blk"), None), P())
    return jax.shard_map(local, mesh=mesh, in_specs=in_specs, out_specs=out_specs, check_vma=False)
```

```python
import functools
import jax
import jax.numpy as jnp
from jax import lax
from jax.experimental import pallas as pl
from jax.experimental.pallas import tpu as pltpu
from jax.sharding import PartitionSpec as P

F32 = jnp.float32
BF16 = jnp.bfloat16
MESH = pl.DeviceIdType.MESH
EDGE = 256
RB = 16
CB = 4
K = 512
PX, PY, PZ = 4, 4, 8


def where_am_i():
    row = lax.axis_index("row")
    blk = lax.axis_index("blk")
    return row // 2, row % 2, blk // PX, blk % PX


class Net:
    def __init__(self, send_sems, recv_sems):
        self.send_sems, self.recv_sems = send_sems, recv_sems
        self.used = 0
        self.z, self.c, self.y, self.x = where_am_i()

    def device(self, dz=0, dc=0, dy=0, dx=0):
        z = lax.rem(self.z + dz + PZ, PZ)
        c = 1 - self.c if dc else self.c
        y = lax.rem(self.y + dy + PY, PY)
        x = lax.rem(self.x + dx + PX, PX)
        return {"row": z * 2 + c, "blk": y * PX + x}

    def greet(self, steps):
        barrier = pltpu.get_barrier_semaphore()
        for step in steps:
            pl.semaphore_signal(barrier, inc=1, device_id=self.device(**step), device_id_type=MESH)
        pl.semaphore_wait(barrier, len(steps))

    def copy(self, src, dst, **step):
        slot = self.used
        self.used += 1
        return pltpu.make_async_remote_copy(
            src_ref=src, dst_ref=dst, send_sem=self.send_sems.at[slot], recv_sem=self.recv_sems.at[slot],
            device_id=self.device(**step), device_id_type=MESH)


NEIGHBOURS = [dict(dx=1), dict(dx=-1), dict(dy=1), dict(dy=-1), dict(dz=1), dict(dz=-1), dict(dc=1)]


def build_dense(slot_ref, tiles, dense):
    @pl.loop(0, RB)
    def _(i):
        for c in range(CB):
            slot = slot_ref[i * CB + c]
            keep = jnp.where(slot >= 0, 1.0, 0.0).astype(BF16)
            dense[i, :, c * EDGE:(c + 1) * EDGE] = tiles[jnp.maximum(slot, 0)] * keep


def slot_table(tile_rows, tile_cols, counts):
    slots = jnp.arange(tile_rows.shape[0], dtype=jnp.int32)
    spot = tile_rows * CB + tile_cols
    hit = (spot[None, :] == jnp.arange(RB * CB)[:, None]) & (slots < counts)[None, :]
    return jnp.max(jnp.where(hit, slots[None, :], -1), axis=1)


HIGH = lax.Precision.HIGHEST


def reach():
    steps = [dict(dc=1)]
    steps += [dict(dx=d) for d in (1, -1, 2)]
    steps += [dict(dy=d) for d in (1, -1, 2)]
    steps += [dict(dz=d) for d in (1, -1, 2, -2, 3, -3, 4)]
    return steps


PANELS = [(i, j) for j in range(4) for i in range(j + 1)]

GR = (512, 1024)


def lane(x, j):
    return jnp.take_along_axis(x, jnp.full(x.shape, j, jnp.int32), axis=1)


def sub(x, i):
    return jnp.broadcast_to(x[i:i + 1, :], x.shape)


def factor_block(S, E):
    rid = lax.broadcasted_iota(jnp.int32, (8, 128), 0)
    lid = lax.broadcasted_iota(jnp.int32, (8, 128), 1)
    E[:] = [(lid == rid + 8 * i).astype(F32) for i in range(16)]
    for g in range(16):
        cols = [lane(S[g], 8 * g + k) for k in range(8)]
        ss, ee = [sub(S[g], k) for k in range(8)], [sub(E[g], k) for k in range(8)]
        a = {(i, k): sub(cols[k], i) for k in range(8) for i in range(k, 8)}
        r, l, m = [None] * 8, {}, {}
        for k in range(8):
            r[k] = lax.rsqrt(a[k, k])
            for i in range(k + 1, 8):
                l[i, k] = a[i, k] * r[k]
            for i in range(k + 1, 8):
                for n in range(k + 1, i + 1):
                    a[i, n] = a[i, n] - l[i, k] * l[n, k]
            m[k, k] = r[k]
            for j in range(k):
                t = l[k, j] * m[j, j]
                for q in range(j + 1, k):
                    t = t + l[k, q] * m[q, j]
                m[k, j] = -(t * r[k])

        def mixed(terms, n):
            value = terms[0] * m[n, 0]
            for k in range(1, n + 1):
                value = value + terms[k] * m[n, k]
            return value

        us, es = [mixed(ss, n) for n in range(8)], [mixed(ee, n) for n in range(8)]
        later = {i: [lane(S[i], 8 * g + k) for k in range(8)] for i in range(g + 1, 16)}
        for i in range(g + 1, 16):
            for n in range(8):
                c = mixed(later[i], n)
                S[i] = S[i] - c * us[n]
                E[i] = E[i] - c * es[n]
        S[g], E[g] = us[0], es[0]
        for n in range(1, 8):
            S[g], E[g] = jnp.where(rid == n, us[n], S[g]), jnp.where(rid == n, es[n], E[g])
        yield CHOL
    S[:] = [jnp.where(lid >= rid + 8 * i, s, 0.0) for i, s in enumerate(S)]


def dot(a, b, dims=((1,), (0,))):
    return lax.dot_general(a, b, (dims, ((), ())), precision=HIGH, preferred_element_type=F32)


def weave(*works):
    queue = [[begin, n, work] for n, (begin, work) in enumerate(works)]
    while queue:
        entry = min(queue)
        try:
            entry[0] += next(entry[2])
        except StopIteration:
            queue.remove(entry)


def power_kernel(slot_ref, tiles_hbm, sketch_ref, basis, factor, image, gram0, gram1, S, inv, tiles, dense, gath, part, pair, chain, ci, acc, far, in1, sum2, in2,
                 gbuf0, gbuf1, gpair, g1, g2, gstage, gz, dma_sem, send_sems, recv_sems):
    net = Net(send_sems, recv_sems)
    load = pltpu.make_async_copy(tiles_hbm, tiles, dma_sem)
    load.start()
    mine = net.y * PX + net.x
    gath[mine] = sketch_ref[...].astype(F32).T.astype(BF16)
    net.greet(reach())
    started = []
    axes = [("dx", "dy"), ("dy", "dx")]

    def start(copy):
        copy.start()
        started.append(copy)
        return copy

    def begin(copy):
        copy.start()
        return copy

    def block_of(h, dp, dq):
        dx, dy = (dp, dq) if h == 0 else (dq, dp)
        return lax.rem(net.y + dy + PY, PY) * PX + lax.rem(net.x + dx + PX, PX)

    def slab(d):
        return lax.rem(net.z + d + PZ, PZ)

    def gather(t):
        base = 256 * t
        arrive = {}
        got = set()

        def go(h, dp, dq, axis, sign, key):
            where = gath.at[block_of(h, dp, dq), pl.ds(base + h * 128, 128), :]
            arrive[key] = net.used
            start(net.copy(where, where, **{axis: sign}))

        def received(h, dp, dq):
            where = gath.at[block_of(h, dp, dq), pl.ds(base + h * 128, 128), :]
            n = arrive[h, dp, dq]
            pltpu.make_async_remote_copy(
                src_ref=where, dst_ref=where, send_sem=send_sems.at[n], recv_sem=recv_sems.at[n],
                device_id=net.device(dx=1), device_id_type=MESH).wait_recv()

        def multiply(dx, dy):
            i = block_of(0, dx, dy)
            block = gath[i, base:base + 256, :]
            for c in range(CB):
                prod = jnp.dot(block, dense[i, :, c * EDGE:(c + 1) * EDGE], preferred_element_type=F32)
                for s in range(2):
                    piece = prod[:, s * 128:(s + 1) * 128]
                    if (dx, dy) == (0, 0):
                        part[2 * c + s, base:base + 256, :] = piece
                    else:
                        part[2 * c + s, base:base + 256, :] += piece

        for h in range(2):
            p, q = axes[h]
            go(h, 0, 0, p, 1, (h, -1, 0))
            go(h, 0, 0, p, -1, (h, 1, 0))
        for h in range(2):
            p, q = axes[h]
            go(h, 0, 0, q, 1, (h, 0, -1))
            go(h, 0, 0, q, -1, (h, 0, 1))
        if t == 0:
            load.wait()
            build_dense(slot_ref, tiles, dense)
        yield GATHER[t][0]
        multiply(0, 0)
        order = [(-1, 0), (1, 0), (0, -1), (0, 1), (2, 0), (-1, -1), (-1, 1), (0, 2), (1, -1), (1, 1), (-1, 2), (2, -1), (2, 1), (1, 2), (2, 2)]
        for dp, dq in order:
            for h in range(2):
                p, q = axes[h]
                received(h, dp, dq)
                if dq == 0:
                    if dp == -1:
                        go(h, dp, 0, p, 1, (h, 2, 0))
                    go(h, dp, 0, q, 1, (h, dp, -1))
                    go(h, dp, 0, q, -1, (h, dp, 1))
                elif dq == -1 and dp in (0, 2):
                    go(h, dp, dq, q, 1, (h, dp, 2))
                elif dq == 1 and dp in (-1, 1):
                    go(h, dp, dq, q, -1, (h, dp, 2))
            got.add((dp, dq))
            if (dq, dp) in got:
                for dx, dy in {(dp, dq): 0, (dq, dp): 0}:
                    multiply(dx, dy)
            yield GATHER[t][1]

    def columns(t):
        base = 256 * t
        own = pl.multiple_of(base + net.c * 128, 128)
        other = pl.multiple_of(base + (1 - net.c) * 128, 128)
        pairs, legs, shared = {}, {}, []

        def merge(d):
            pairs[d].wait_recv()
            part[slab(d), pl.ds(own, 128), :] += pair[t, slab(d)]

        def leg(name, d, u, slot, dz):
            src = part.at[slab(d), pl.ds(own, 128) if u is None else pl.ds(pl.multiple_of(own + u * 64, 64), 64), :]
            dst = chain.at[t, slot] if u is None else chain.at[t, slot, pl.ds(0, 64), :]
            legs[name] = start(net.copy(src, dst, dz=dz))

        for d in (4, 3, -3, 1, -1, 2, -2, 0):
            pairs[d] = start(net.copy(part.at[slab(d), pl.ds(other, 128), :], pair.at[t, slab(d)], dc=1))
        yield ZPAIR
        merge(4)
        leg((4, 1), 4, 0, 0, 2)
        leg((4, -1), 4, 1, 1, -2)
        merge(3)
        leg((3, 1), 3, None, 2, 1)
        merge(-3)
        leg((3, -1), -3, None, 3, -1)
        merge(1)
        leg((1, 1), 1, None, 4, 1)
        merge(-1)
        leg((1, -1), -1, None, 5, -1)
        merge(2)
        merge(-2)
        yield ZFAR
        for n, sign in enumerate((1, -1)):
            legs[3, sign].wait_recv()
            part[slab(2 * sign), pl.ds(own, 128), :] += chain[t, 2 + n]
            legs[4, sign].wait_recv()
            part[slab(2 * sign), pl.ds(pl.multiple_of(own + n * 64, 64), 64), :] += chain[t, n, 0:64, :]
            leg((2, sign), 2 * sign, None, 6 + n, 2 * sign)
        merge(0)
        yield ZNEAR
        value = part[net.z, pl.ds(own, 128), :]
        for n, sign in enumerate((1, -1)):
            legs[1, sign].wait_recv()
            value = value + chain[t, 4 + n]
        yield ZLAST
        for n, sign in enumerate((1, -1)):
            legs[2, sign].wait_recv()
            value = value + chain[t, 6 + n]

        def place(d, u=None):
            at = slab(d) * 128 + (0 if u is None else u * 64)
            return ci.at[2 * t + net.c, pl.ds(pl.multiple_of(at, 64), 128 if u is None else 64), :]

        def send(d, dz, u=None):
            return start(net.copy(place(d, u), place(d, u), dz=dz))

        def share(d, u=None):
            shared.append(start(net.copy(place(d, u), place(d, u), dc=1)))

        ci[2 * t + net.c, pl.ds(pl.multiple_of(net.z * 128, 128), 128), :] = value.T.astype(BF16)
        two = {sign: send(0, 2 * sign) for sign in (1, -1)}
        one = {sign: send(0, sign) for sign in (1, -1)}
        share(0)
        yield ZRING
        three, four = {}, {}
        for n, sign in enumerate((1, -1)):
            two[sign].wait_recv()
            four[sign] = send(-2 * sign, 2 * sign, n)
            three[sign] = send(-2 * sign, sign)
            share(-2 * sign)
        for sign in (1, -1):
            one[sign].wait_recv()
            share(-sign)
        yield ZRING
        for sign in (1, -1):
            three[sign].wait_recv()
            share(-3 * sign)
        for n, sign in enumerate((1, -1)):
            four[sign].wait_recv()
            share(4, n)
        yield ZSHARE
        for copy in shared:
            copy.wait_recv()

    def rows_out(t):
        moves, moves2, made = {}, {}, set()
        QS = (2, 1, -1, 0)

        def product(h, dp, dq):
            spot = (dp, dq) if h == 0 else (dq, dp)
            i = block_of(h, dp, dq)
            if spot not in made:
                made.add(spot)
                right = jnp.concatenate([ci[2 * t], ci[2 * t + 1]], axis=1)
                acc[t, i] = jnp.dot(dense[i], right, preferred_element_type=F32)
            return acc[t, i, :, h * 128:(h + 1) * 128]

        def send1(h, dp, dq, sign, value):
            n = len(moves)
            far[t, n] = value.astype(BF16)
            moves[h, dp, dq] = start(net.copy(far.at[t, n], in1.at[t, n], **{axes[h][0]: sign})), n

        def via(dq):
            return 1 if dq in (0, 2) else -1

        def send2(h, dq, piece, sign):
            n = len(moves2)
            moves2[h, dq, piece] = start(net.copy(sum2.at[t, h, dq % 4, pl.ds(piece * 128, 128), :], in2.at[t, n], **{axes[h][1]: sign})), n

        for dq in QS:
            for h in range(2):
                send1(h, 2, dq, via(dq), product(h, 2, dq))
            yield PROD
        for dq in QS:
            for h in range(2):
                s = -via(dq)
                send1(h, s, dq, s, product(h, s, dq))
            yield PROD
        for dq in QS:
            for h in range(2):
                product(h, via(dq), dq)
                product(h, 0, dq)
            yield RS1[QS.index(dq)]
            for h in range(2):
                s = via(dq)
                copy, n = moves[h, 2, dq]
                copy.wait_recv()
                send1(h, s, dq, s, product(h, s, dq) + in1[t, n].astype(F32))
        for dq in QS:
            yield RS2[QS.index(dq)]
            for h in range(2):
                value = product(h, 0, dq)
                for s in (-via(dq), via(dq)):
                    copy, n = moves[h, s, dq]
                    copy.wait_recv()
                    value = value + in1[t, n].astype(F32)
                sum2[t, h, dq % 4] = value
                if dq == 2:
                    send2(h, 2, 0, 1)
                    send2(h, 2, 1, -1)
                elif dq != 0:
                    send2(h, dq, 0 if dq == -1 else 1, dq)
        for dq in (1, -1):
            yield RS3[dq == -1]
            for h in range(2):
                through = 0 if dq == 1 else 1
                copy, n = moves2[h, 2, through]
                copy.wait_recv()
                sum2[t, h, dq % 4, through * 128:(through + 1) * 128, :] += in2[t, n]
                send2(h, dq, through, dq)
        yield RS4
        for h in range(2):
            for piece in range(2):
                value = sum2[t, h, 0, piece * 128:(piece + 1) * 128, :]
                for dq in (1, -1):
                    copy, n = moves2[h, dq, piece]
                    copy.wait_recv()
                    value = value + in2[t, n]
                image[piece * 128:(piece + 1) * 128, t * 256 + h * 128:t * 256 + (h + 1) * 128] = value

    def moments(t):
        size = GR[t]
        gbuf, out = (gbuf0, gram0) if t == 0 else (gbuf1, gram1)
        scale = 1.0 / (lax.axis_size("row") * lax.axis_size("blk") * EDGE)
        panels = [p for p in PANELS if p[1] // 2 == t]
        for n, (i, j) in enumerate(panels):
            gbuf[n * 128:(n + 1) * 128, :] = lax.dot_general(
                image[:, i * 128:(i + 1) * 128], image[:, j * 128:(j + 1) * 128], (((0,), (0,)), ((), ())),
                precision=HIGH, preferred_element_type=F32) * scale
        gbuf[size - 128:, :] = jnp.zeros((128, 128), F32)
        half, quarter, first, second = size // 2, size // 4, size // 16, size // 64
        base = pl.multiple_of(net.c * half, 256)
        twin = start(net.copy(gbuf.at[pl.ds(pl.multiple_of((1 - net.c) * half, 256), half), :], gpair.at[pl.ds(t * 256, half), :], dc=1))
        yield GM1[t]
        twin.wait_recv()
        gbuf[pl.ds(base, half), :] += gpair[t * 256:t * 256 + half, :]

        def cut(at, pos, d, step):
            return pl.ds(pl.multiple_of(at + lax.rem(pos + d + 4, 4) * step, 8), step)

        place = (net.x, net.y)
        ats = [base + v * quarter for v in range(2)]
        for level, step in enumerate((first, second)):
            copies = {}
            for d in (2, 1, -1):
                for v in range(2):
                    n = {2: 0, 1: 1, -1: 2}[d]
                    land = g1.at[t, v, n, pl.ds(0, step), :] if level == 0 else g2.at[t, v, n, pl.ds(0, step), :]
                    axis = axes[v][level]
                    copies[v, n] = start(net.copy(gbuf.at[cut(ats[v], place[(v + level) % 2], d, step), :], land, **{axis: d}))
            yield GM2[t]
            for v in range(2):
                here = cut(ats[v], place[(v + level) % 2], 0, step)
                value = gbuf[here, :]
                for n in range(3):
                    copies[v, n].wait_recv()
                    value = value + (g1 if level == 0 else g2)[t, v, n, 0:step, :]
                if level == 0:
                    gbuf[here, :] = value
                else:
                    gstage[t, v * second:(v + 1) * second, :] = value
                ats[v] = pl.multiple_of(ats[v] + place[(v + level) % 2] * step, 8)
        both = 2 * second
        offsets = (4, 3, -3, 2, -2, 1, -1, 0)
        copies = [start(net.copy(gstage.at[t, pl.ds(0, both), :], gz.at[t, n, pl.ds(0, both), :], dz=d)) for n, d in enumerate(offsets[:-1])]
        gz[t, 7, 0:both, :] = gstage[t, 0:both, :]
        yield GM3[t]
        for copy in copies:
            copy.wait_recv()
        value = None
        for spot in range(PZ):
            d = lax.rem(net.z - spot + PZ, PZ)
            at = 0
            for n, o in enumerate(offsets):
                at = at + jnp.where(d == o % PZ, n, 0)
            term = gz[t, at, 0:both, :]
            value = term if value is None else value + term
        for v in range(2):
            out[pl.ds(ats[v], second), :] = value[v * second:(v + 1) * second, :]
        for level, step in ((1, second), (0, first)):
            copies = []
            for v in range(2):
                if level == 0:
                    ats[v] = base + v * quarter + place[v % 2] * first
                where = out.at[pl.ds(pl.multiple_of(ats[v], 8), step), :]
                for d in (2, 1, -1):
                    copies.append(start(net.copy(where, where, **{axes[v][level]: d})))
            yield GM2[t]
            for copy in copies:
                copy.wait_recv()
        where = out.at[pl.ds(base, half), :]
        twin = start(net.copy(where, where, dc=1))
        yield GM1[t]
        twin.wait_recv()

    index = {p: n for n, p in enumerate(PANELS)}

    def span(b):
        return slice(b * 128, (b + 1) * 128)

    def panel(i, j):
        n = index[i, j]
        return gram0[span(n), :] if n < 3 else gram1[span(n - 3), :]

    def reduced(i, j, upto):
        value = panel(i, j)
        for k in range(upto):
            value = value - dot(factor[span(k), span(i)], factor[span(k), span(j)], ((0,), (0,)))
        return value

    def solve(b):
        for i in range(b):
            factor[span(b), span(i)] = jnp.zeros((128, 128), F32)
        if b == 2:
            for j in (2, 3):
                for i in (0, 1):
                    factor[span(i), span(j)] = dot(inv[i], reduced(i, j, i))
        yield CHOL
        S[...] = reduced(b, b, b)
        value = image[:, span(b)]
        for k in range(b):
            value = value - dot(basis[:, span(k)], factor[span(k), span(b)])
        yield CHOL
        rows, e = [S[8 * g:8 * g + 8, :] for g in range(16)], []
        yield from factor_block(rows, e)
        for g in range(16):
            factor[b * 128 + 8 * g:b * 128 + 8 * g + 8, span(b)] = rows[g]
            inv[b, 8 * g:8 * g + 8, :] = e[g]
        yield CHOL
        if b % 2 == 0:
            factor[span(b), span(b + 1)] = dot(inv[b], reduced(b, b + 1, b))
        yield CHOL
        basis[:, span(b)] = dot(value, inv[b], ((1,), (1,)))

    def process(t):
        yield from gather(t)
        yield from columns(t)
        yield from rows_out(t)
        yield from moments(t)

        if t == 0:
            yield from solve(0)
            yield from solve(1)

    weave((0.0, process(0)), (SECOND, process(1)))
    weave((0.0, solve(2)))
    weave((0.0, solve(3)))
    for copy in started:
        copy.wait_send()


SECOND = 20.0
GATHER = ((9.0, 1.1), (5.0, 1.3))
ZPAIR, ZFAR, ZNEAR, ZLAST, ZRING, ZSHARE = 3.5, 6.5, 1.0, 5.0, 4.5, 2.0
PROD = 0.6
RS1, RS2, RS3, RS4 = (0.6, 1.2, 1.2, 1.2), (2.5, 1.2, 1.2, 1.2), (1.5, 0.7), 2.5
GM1, GM2, GM3 = (3.0, 2.0), (4.5, 3.0), (6.5, 6.0)
CHOL = 0.4


def power_step(slots, tiles, sketch):
    vmem = pl.BlockSpec(memory_space=pltpu.VMEM)
    return pl.pallas_call(
        power_kernel,
        name="power_step",
        out_shape=[jax.ShapeDtypeStruct((EDGE, K), F32), jax.ShapeDtypeStruct((K, K), F32)],
        in_specs=[pl.BlockSpec(memory_space=pltpu.SMEM), pl.BlockSpec(memory_space=pl.ANY), vmem],
        out_specs=[vmem, vmem],
        scratch_shapes=[
            pltpu.VMEM((EDGE, K), F32),
            pltpu.VMEM((GR[0], 128), F32),
            pltpu.VMEM((GR[1], 128), F32),
            pltpu.VMEM((128, 128), F32),
            pltpu.VMEM((4, 128, 128), F32),
            pltpu.VMEM((32, EDGE, EDGE), BF16),
            pltpu.VMEM((RB, EDGE, CB * EDGE), BF16),
            pltpu.VMEM((RB, K, EDGE), BF16),
            pltpu.VMEM((8, K, 128), F32),
            pltpu.VMEM((2, 8, 128, 128), F32),
            pltpu.VMEM((2, 8, 128, 128), F32),
            pltpu.VMEM((4, 1024, 128), BF16),
            pltpu.VMEM((2, RB, EDGE, EDGE), F32),
            pltpu.VMEM((2, 24, EDGE, 128), BF16),
            pltpu.VMEM((2, 24, EDGE, 128), BF16),
            pltpu.VMEM((2, 2, 4, EDGE, 128), F32),
            pltpu.VMEM((2, 12, 128, 128), F32),
            pltpu.VMEM((GR[0], 128), F32),
            pltpu.VMEM((GR[1], 128), F32),
            pltpu.VMEM((768, 128), F32),
            pltpu.VMEM((2, 2, 3, 64, 128), F32),
            pltpu.VMEM((2, 2, 3, 16, 128), F32),
            pltpu.VMEM((2, 32, 128), F32),
            pltpu.VMEM((2, 8, 32, 128), F32),
            pltpu.SemaphoreType.DMA,
            pltpu.SemaphoreType.DMA((320,)),
            pltpu.SemaphoreType.DMA((320,)),
        ],
        compiler_params=pltpu.CompilerParams(collective_id=0, has_side_effects=True, vmem_limit_bytes=60 << 20),
    )(slots, tiles, sketch)


def hand_kernel(basis, factor, basis_out, factor_out, sems):
    copies = [pltpu.make_async_copy(basis.at[pl.ds(128 * n, 128), :], basis_out.at[pl.ds(128 * n, 128), :], sems.at[n]) for n in range(2)]
    copies += [pltpu.make_async_copy(factor.at[pl.ds(128 * n, 128), :], factor_out.at[pl.ds(128 * n, 128), :], sems.at[2 + n]) for n in range(4)]
    for copy in copies:
        copy.start()
    for copy in copies:
        copy.wait()


def hand_over(basis, factor):
    anywhere = pl.BlockSpec(memory_space=pl.ANY)
    return pl.pallas_call(
        hand_kernel,
        name="hand_over",
        out_shape=[jax.ShapeDtypeStruct((EDGE, K), F32), jax.ShapeDtypeStruct((K, K), F32)],
        in_specs=[anywhere, anywhere],
        out_specs=[anywhere, anywhere],
        scratch_shapes=[pltpu.SemaphoreType.DMA((6,))],
        compiler_params=pltpu.CompilerParams(vmem_limit_bytes=60 << 20),
    )(basis, factor)


def local(tiles, tile_rows, tile_cols, counts, sketch):
    blocks = tiles[0, 0]
    slots = slot_table(tile_rows[0, 0], tile_cols[0, 0], counts[0, 0])
    return hand_over(*power_step(slots, blocks, sketch))


def solution(mesh):
    in_specs = (
        P("row", "blk", None, None, None),
        P("row", "blk", None),
        P("row", "blk", None),
        P("row", "blk"),
        P(("row", "blk"), None),
    )
    out_specs = (P(("row", "blk"), None), P())
    return jax.shard_map(local, mesh=mesh, in_specs=in_specs, out_specs=out_specs, check_vma=False)
```

```python
import functools
import jax
import jax.numpy as jnp
from jax import lax
from jax.experimental import pallas as pl
from jax.experimental.pallas import tpu as pltpu
from jax.sharding import PartitionSpec as P

F32 = jnp.float32
BF16 = jnp.bfloat16
MESH = pl.DeviceIdType.MESH
EDGE = 256
RB = 16
CB = 4
K = 512
PX, PY, PZ = 4, 4, 8


def where_am_i():
    row = lax.axis_index("row")
    blk = lax.axis_index("blk")
    return row // 2, row % 2, blk // PX, blk % PX


class Net:
    def __init__(self, send_sems, recv_sems):
        self.send_sems, self.recv_sems = send_sems, recv_sems
        self.used = 0
        self.z, self.c, self.y, self.x = where_am_i()

    def device(self, dz=0, dc=0, dy=0, dx=0):
        z = lax.rem(self.z + dz + PZ, PZ)
        c = 1 - self.c if dc else self.c
        y = lax.rem(self.y + dy + PY, PY)
        x = lax.rem(self.x + dx + PX, PX)
        return {"row": z * 2 + c, "blk": y * PX + x}

    def greet(self, steps):
        barrier = pltpu.get_barrier_semaphore()
        for step in steps:
            pl.semaphore_signal(barrier, inc=1, device_id=self.device(**step), device_id_type=MESH)
        pl.semaphore_wait(barrier, len(steps))

    def copy(self, src, dst, **step):
        slot = self.used
        self.used += 1
        return pltpu.make_async_remote_copy(
            src_ref=src, dst_ref=dst, send_sem=self.send_sems.at[slot], recv_sem=self.recv_sems.at[slot],
            device_id=self.device(**step), device_id_type=MESH)


NEIGHBOURS = [dict(dx=1), dict(dx=-1), dict(dy=1), dict(dy=-1), dict(dz=1), dict(dz=-1), dict(dc=1)]


def build_dense(slot_ref, tiles, dense):
    @pl.loop(0, RB)
    def _(i):
        for c in range(CB):
            slot = slot_ref[i * CB + c]
            keep = jnp.where(slot >= 0, 1.0, 0.0).astype(BF16)
            dense[i, :, c * EDGE:(c + 1) * EDGE] = tiles[jnp.maximum(slot, 0)] * keep


def slot_table(tile_rows, tile_cols, counts):
    slots = jnp.arange(tile_rows.shape[0], dtype=jnp.int32)
    spot = tile_rows * CB + tile_cols
    hit = (spot[None, :] == jnp.arange(RB * CB)[:, None]) & (slots < counts)[None, :]
    return jnp.max(jnp.where(hit, slots[None, :], -1), axis=1)


HIGH = lax.Precision.HIGHEST


def reach():
    steps = [dict(dc=1)]
    steps += [dict(dx=d) for d in (1, -1, 2)]
    steps += [dict(dy=d) for d in (1, -1, 2)]
    steps += [dict(dz=d) for d in (1, -1, 2, -2, 3, -3, 4)]
    return steps


PANELS = [(i, j) for j in range(4) for i in range(j + 1)]

GR = (512, 1024)


def lane(x, j):
    return jnp.take_along_axis(x, jnp.full(x.shape, j, jnp.int32), axis=1)


def sub(x, i):
    return jnp.broadcast_to(x[i:i + 1, :], x.shape)


def factor_block(S, E):
    rid = lax.broadcasted_iota(jnp.int32, (8, 128), 0)
    lid = lax.broadcasted_iota(jnp.int32, (8, 128), 1)
    E[:] = [(lid == rid + 8 * i).astype(F32) for i in range(16)]
    for g in range(16):
        cols = [lane(S[g], 8 * g + k) for k in range(8)]
        ss, ee = [sub(S[g], k) for k in range(8)], [sub(E[g], k) for k in range(8)]
        a = {(i, k): sub(cols[k], i) for k in range(8) for i in range(k, 8)}
        r, l, m = [None] * 8, {}, {}
        for k in range(8):
            r[k] = lax.rsqrt(a[k, k])
            for i in range(k + 1, 8):
                l[i, k] = a[i, k] * r[k]
            for i in range(k + 1, 8):
                for n in range(k + 1, i + 1):
                    a[i, n] = a[i, n] - l[i, k] * l[n, k]
            m[k, k] = r[k]
            for j in range(k):
                t = l[k, j] * m[j, j]
                for q in range(j + 1, k):
                    t = t + l[k, q] * m[q, j]
                m[k, j] = -(t * r[k])

        def mixed(terms, n):
            value = terms[0] * m[n, 0]
            for k in range(1, n + 1):
                value = value + terms[k] * m[n, k]
            return value

        us, es = [mixed(ss, n) for n in range(8)], [mixed(ee, n) for n in range(8)]
        later = {i: [lane(S[i], 8 * g + k) for k in range(8)] for i in range(g + 1, 16)}
        for i in range(g + 1, 16):
            for n in range(8):
                c = mixed(later[i], n)
                S[i] = S[i] - c * us[n]
                E[i] = E[i] - c * es[n]
        S[g], E[g] = us[0], es[0]
        for n in range(1, 8):
            S[g], E[g] = jnp.where(rid == n, us[n], S[g]), jnp.where(rid == n, es[n], E[g])
        yield CHOL
    S[:] = [jnp.where(lid >= rid + 8 * i, s, 0.0) for i, s in enumerate(S)]


def dot(a, b, dims=((1,), (0,))):
    return lax.dot_general(a, b, (dims, ((), ())), precision=HIGH, preferred_element_type=F32)


def weave(*works):
    queue = [[begin, n, work] for n, (begin, work) in enumerate(works)]
    while queue:
        entry = min(queue)
        try:
            entry[0] += next(entry[2])
        except StopIteration:
            queue.remove(entry)


def power_kernel(slot_ref, tiles_hbm, sketch_ref, basis, factor, image, gram0, gram1, S, inv, tiles, dense, gath, part, pair, chain, ci, acc, far, in1, sum2, in2,
                 gbuf0, gbuf1, gpair, g1, g2, gstage, gz, dma_sem, send_sems, recv_sems):
    net = Net(send_sems, recv_sems)
    load = pltpu.make_async_copy(tiles_hbm, tiles, dma_sem)
    load.start()
    mine = net.y * PX + net.x
    gath[mine] = sketch_ref[...].astype(F32).T.astype(BF16)
    net.greet(reach())
    started = []
    axes = [("dx", "dy"), ("dy", "dx")]

    def start(copy):
        copy.start()
        started.append(copy)
        return copy

    def begin(copy):
        copy.start()
        return copy

    def block_of(h, dp, dq):
        dx, dy = (dp, dq) if h == 0 else (dq, dp)
        return lax.rem(net.y + dy + PY, PY) * PX + lax.rem(net.x + dx + PX, PX)

    def slab(d):
        return lax.rem(net.z + d + PZ, PZ)

    def gather(t):
        base = 256 * t
        arrive = {}
        got = set()

        def go(h, dp, dq, axis, sign, key):
            where = gath.at[block_of(h, dp, dq), pl.ds(base + h * 128, 128), :]
            arrive[key] = net.used
            start(net.copy(where, where, **{axis: sign}))

        def received(h, dp, dq):
            where = gath.at[block_of(h, dp, dq), pl.ds(base + h * 128, 128), :]
            n = arrive[h, dp, dq]
            pltpu.make_async_remote_copy(
                src_ref=where, dst_ref=where, send_sem=send_sems.at[n], recv_sem=recv_sems.at[n],
                device_id=net.device(dx=1), device_id_type=MESH).wait_recv()

        def multiply(dx, dy):
            i = block_of(0, dx, dy)
            block = gath[i, base:base + 256, :]
            for c in range(CB):
                prod = jnp.dot(block, dense[i, :, c * EDGE:(c + 1) * EDGE], preferred_element_type=F32)
                for s in range(2):
                    piece = prod[:, s * 128:(s + 1) * 128]
                    if (dx, dy) == (0, 0):
                        part[2 * c + s, base:base + 256, :] = piece
                    else:
                        part[2 * c + s, base:base + 256, :] += piece

        for h in range(2):
            p, q = axes[h]
            go(h, 0, 0, p, 1, (h, -1, 0))
            go(h, 0, 0, p, -1, (h, 1, 0))
        for h in range(2):
            p, q = axes[h]
            go(h, 0, 0, q, 1, (h, 0, -1))
            go(h, 0, 0, q, -1, (h, 0, 1))
        if t == 0:
            load.wait()
            build_dense(slot_ref, tiles, dense)
        yield GATHER[t][0]
        multiply(0, 0)
        order = [(-1, 0), (1, 0), (0, -1), (0, 1), (2, 0), (-1, -1), (-1, 1), (0, 2), (1, -1), (1, 1), (-1, 2), (2, -1), (2, 1), (1, 2), (2, 2)]
        for dp, dq in order:
            for h in range(2):
                p, q = axes[h]
                received(h, dp, dq)
                if dq == 0:
                    if dp == -1:
                        go(h, dp, 0, p, 1, (h, 2, 0))
                    go(h, dp, 0, q, 1, (h, dp, -1))
                    go(h, dp, 0, q, -1, (h, dp, 1))
                elif dq == -1 and dp in (0, 2):
                    go(h, dp, dq, q, 1, (h, dp, 2))
                elif dq == 1 and dp in (-1, 1):
                    go(h, dp, dq, q, -1, (h, dp, 2))
            got.add((dp, dq))
            if (dq, dp) in got:
                for dx, dy in {(dp, dq): 0, (dq, dp): 0}:
                    multiply(dx, dy)
            yield GATHER[t][1]

    def columns(t):
        base = 256 * t
        own = pl.multiple_of(base + net.c * 128, 128)
        other = pl.multiple_of(base + (1 - net.c) * 128, 128)
        pairs, legs, shared = {}, {}, []

        def merge(d):
            pairs[d].wait_recv()
            part[slab(d), pl.ds(own, 128), :] += pair[t, slab(d)]

        def leg(name, d, u, slot, dz):
            src = part.at[slab(d), pl.ds(own, 128) if u is None else pl.ds(pl.multiple_of(own + u * 64, 64), 64), :]
            dst = chain.at[t, slot] if u is None else chain.at[t, slot, pl.ds(0, 64), :]
            legs[name] = start(net.copy(src, dst, dz=dz))

        for d in (4, 3, -3, 1, -1, 2, -2, 0):
            pairs[d] = start(net.copy(part.at[slab(d), pl.ds(other, 128), :], pair.at[t, slab(d)], dc=1))
        yield ZPAIR
        merge(4)
        leg((4, 1), 4, 0, 0, 2)
        leg((4, -1), 4, 1, 1, -2)
        merge(3)
        leg((3, 1), 3, None, 2, 1)
        merge(-3)
        leg((3, -1), -3, None, 3, -1)
        merge(1)
        leg((1, 1), 1, None, 4, 1)
        merge(-1)
        leg((1, -1), -1, None, 5, -1)
        merge(2)
        merge(-2)
        yield ZFAR
        for n, sign in enumerate((1, -1)):
            legs[3, sign].wait_recv()
            part[slab(2 * sign), pl.ds(own, 128), :] += chain[t, 2 + n]
            legs[4, sign].wait_recv()
            part[slab(2 * sign), pl.ds(pl.multiple_of(own + n * 64, 64), 64), :] += chain[t, n, 0:64, :]
            leg((2, sign), 2 * sign, None, 6 + n, 2 * sign)
        merge(0)
        yield ZNEAR
        value = part[net.z, pl.ds(own, 128), :]
        for n, sign in enumerate((1, -1)):
            legs[1, sign].wait_recv()
            value = value + chain[t, 4 + n]
        yield ZLAST
        for n, sign in enumerate((1, -1)):
            legs[2, sign].wait_recv()
            value = value + chain[t, 6 + n]

        def place(d, u=None):
            at = slab(d) * 128 + (0 if u is None else u * 64)
            return ci.at[2 * t + net.c, pl.ds(pl.multiple_of(at, 64), 128 if u is None else 64), :]

        def send(d, dz, u=None):
            return start(net.copy(place(d, u), place(d, u), dz=dz))

        def share(d, u=None):
            shared.append(start(net.copy(place(d, u), place(d, u), dc=1)))

        ci[2 * t + net.c, pl.ds(pl.multiple_of(net.z * 128, 128), 128), :] = value.T.astype(BF16)
        two = {sign: send(0, 2 * sign) for sign in (1, -1)}
        one = {sign: send(0, sign) for sign in (1, -1)}
        share(0)
        yield ZRING
        three, four = {}, {}
        for n, sign in enumerate((1, -1)):
            two[sign].wait_recv()
            four[sign] = send(-2 * sign, 2 * sign, n)
            three[sign] = send(-2 * sign, sign)
            share(-2 * sign)
        for sign in (1, -1):
            one[sign].wait_recv()
            share(-sign)
        yield ZRING
        for sign in (1, -1):
            three[sign].wait_recv()
            share(-3 * sign)
        for n, sign in enumerate((1, -1)):
            four[sign].wait_recv()
            share(4, n)
        yield ZSHARE
        for copy in shared:
            copy.wait_recv()

    def rows_out(t):
        moves, moves2, made = {}, {}, set()
        QS = (2, 1, -1, 0)

        def product(h, dp, dq):
            spot = (dp, dq) if h == 0 else (dq, dp)
            i = block_of(h, dp, dq)
            if spot not in made:
                made.add(spot)
                right = jnp.concatenate([ci[2 * t], ci[2 * t + 1]], axis=1)
                acc[t, i] = jnp.dot(dense[i], right, preferred_element_type=F32)
            return acc[t, i, :, h * 128:(h + 1) * 128]

        def send1(h, dp, dq, sign, value):
            n = len(moves)
            far[t, n] = value.astype(BF16)
            moves[h, dp, dq] = start(net.copy(far.at[t, n], in1.at[t, n], **{axes[h][0]: sign})), n

        def via(dq):
            return 1 if dq in (0, 2) else -1

        def send2(h, dq, piece, sign):
            n = len(moves2)
            moves2[h, dq, piece] = start(net.copy(sum2.at[t, h, dq % 4, pl.ds(piece * 128, 128), :], in2.at[t, n], **{axes[h][1]: sign})), n

        for dq in QS:
            for h in range(2):
                send1(h, 2, dq, via(dq), product(h, 2, dq))
            yield PROD
        for dq in QS:
            for h in range(2):
                s = -via(dq)
                send1(h, s, dq, s, product(h, s, dq))
            yield PROD
        for dq in QS:
            for h in range(2):
                product(h, via(dq), dq)
                product(h, 0, dq)
            yield RS1[QS.index(dq)]
            for h in range(2):
                s = via(dq)
                copy, n = moves[h, 2, dq]
                copy.wait_recv()
                send1(h, s, dq, s, product(h, s, dq) + in1[t, n].astype(F32))
        for dq in QS:
            yield RS2[QS.index(dq)]
            for h in range(2):
                value = product(h, 0, dq)
                for s in (-via(dq), via(dq)):
                    copy, n = moves[h, s, dq]
                    copy.wait_recv()
                    value = value + in1[t, n].astype(F32)
                sum2[t, h, dq % 4] = value
                if dq == 2:
                    send2(h, 2, 0, 1)
                    send2(h, 2, 1, -1)
                elif dq != 0:
                    send2(h, dq, 0 if dq == -1 else 1, dq)
        for dq in (1, -1):
            yield RS3[dq == -1]
            for h in range(2):
                through = 0 if dq == 1 else 1
                copy, n = moves2[h, 2, through]
                copy.wait_recv()
                sum2[t, h, dq % 4, through * 128:(through + 1) * 128, :] += in2[t, n]
                send2(h, dq, through, dq)
        yield RS4
        for h in range(2):
            for piece in range(2):
                value = sum2[t, h, 0, piece * 128:(piece + 1) * 128, :]
                for dq in (1, -1):
                    copy, n = moves2[h, dq, piece]
                    copy.wait_recv()
                    value = value + in2[t, n]
                image[piece * 128:(piece + 1) * 128, t * 256 + h * 128:t * 256 + (h + 1) * 128] = value

    def moments(t):
        size = GR[t]
        gbuf, out = (gbuf0, gram0) if t == 0 else (gbuf1, gram1)
        scale = 1.0 / (lax.axis_size("row") * lax.axis_size("blk") * EDGE)
        panels = [p for p in PANELS if p[1] // 2 == t]
        for n, (i, j) in enumerate(panels):
            gbuf[n * 128:(n + 1) * 128, :] = lax.dot_general(
                image[:, i * 128:(i + 1) * 128], image[:, j * 128:(j + 1) * 128], (((0,), (0,)), ((), ())),
                precision=HIGH, preferred_element_type=F32) * scale
        gbuf[size - 128:, :] = jnp.zeros((128, 128), F32)
        half, quarter, first, second = size // 2, size // 4, size // 16, size // 64
        base = pl.multiple_of(net.c * half, 256)
        twin = start(net.copy(gbuf.at[pl.ds(pl.multiple_of((1 - net.c) * half, 256), half), :], gpair.at[pl.ds(t * 256, half), :], dc=1))
        yield GM1[t]
        twin.wait_recv()
        gbuf[pl.ds(base, half), :] += gpair[t * 256:t * 256 + half, :]

        def cut(at, pos, d, step):
            return pl.ds(pl.multiple_of(at + lax.rem(pos + d + 4, 4) * step, 8), step)

        place = (net.x, net.y)
        ats = [base + v * quarter for v in range(2)]
        for level, step in enumerate((first, second)):
            copies = {}
            for d in (2, 1, -1):
                for v in range(2):
                    n = {2: 0, 1: 1, -1: 2}[d]
                    land = g1.at[t, v, n, pl.ds(0, step), :] if level == 0 else g2.at[t, v, n, pl.ds(0, step), :]
                    axis = axes[v][level]
                    copies[v, n] = start(net.copy(gbuf.at[cut(ats[v], place[(v + level) % 2], d, step), :], land, **{axis: d}))
            yield GM2[t]
            for v in range(2):
                here = cut(ats[v], place[(v + level) % 2], 0, step)
                value = gbuf[here, :]
                for n in range(3):
                    copies[v, n].wait_recv()
                    value = value + (g1 if level == 0 else g2)[t, v, n, 0:step, :]
                if level == 0:
                    gbuf[here, :] = value
                else:
                    gstage[t, v * second:(v + 1) * second, :] = value
                ats[v] = pl.multiple_of(ats[v] + place[(v + level) % 2] * step, 8)
        both = 2 * second
        offsets = (4, 3, -3, 2, -2, 1, -1, 0)
        copies = [start(net.copy(gstage.at[t, pl.ds(0, both), :], gz.at[t, n, pl.ds(0, both), :], dz=d)) for n, d in enumerate(offsets[:-1])]
        gz[t, 7, 0:both, :] = gstage[t, 0:both, :]
        yield GM3[t]
        for copy in copies:
            copy.wait_recv()
        value = None
        for spot in range(PZ):
            d = lax.rem(net.z - spot + PZ, PZ)
            at = 0
            for n, o in enumerate(offsets):
                at = at + jnp.where(d == o % PZ, n, 0)
            term = gz[t, at, 0:both, :]
            value = term if value is None else value + term
        for v in range(2):
            out[pl.ds(ats[v], second), :] = value[v * second:(v + 1) * second, :]
        for level, step in ((1, second), (0, first)):
            copies = []
            for v in range(2):
                if level == 0:
                    ats[v] = base + v * quarter + place[v % 2] * first
                where = out.at[pl.ds(pl.multiple_of(ats[v], 8), step), :]
                for d in (2, 1, -1):
                    copies.append(start(net.copy(where, where, **{axes[v][level]: d})))
            yield GM2[t]
            for copy in copies:
                copy.wait_recv()
        where = out.at[pl.ds(base, half), :]
        twin = start(net.copy(where, where, dc=1))
        yield GM1[t]
        twin.wait_recv()

    index = {p: n for n, p in enumerate(PANELS)}

    def span(b):
        return slice(b * 128, (b + 1) * 128)

    def panel(i, j):
        n = index[i, j]
        return gram0[span(n), :] if n < 3 else gram1[span(n - 3), :]

    def reduced(i, j, upto):
        value = panel(i, j)
        for k in range(upto):
            value = value - dot(factor[span(k), span(i)], factor[span(k), span(j)], ((0,), (0,)))
        return value

    def solve(b):
        for i in range(b):
            factor[span(b), span(i)] = jnp.zeros((128, 128), F32)
        if b == 2:
            for j in (2, 3):
                for i in (0, 1):
                    factor[span(i), span(j)] = dot(inv[i], reduced(i, j, i))
        yield CHOL
        S[...] = reduced(b, b, b)
        value = image[:, span(b)]
        for k in range(b):
            value = value - dot(basis[:, span(k)], factor[span(k), span(b)])
        yield CHOL
        rows, e = [S[8 * g:8 * g + 8, :] for g in range(16)], []
        yield from factor_block(rows, e)
        for g in range(16):
            factor[b * 128 + 8 * g:b * 128 + 8 * g + 8, span(b)] = rows[g]
            inv[b, 8 * g:8 * g + 8, :] = e[g]
        yield CHOL
        if b % 2 == 0:
            factor[span(b), span(b + 1)] = dot(inv[b], reduced(b, b + 1, b))
        yield CHOL
        basis[:, span(b)] = dot(value, inv[b], ((1,), (1,)))

    def process(t):
        yield from gather(t)
        yield from columns(t)
        yield from rows_out(t)
        yield from moments(t)

        if t == 0:
            yield from solve(0)
            yield from solve(1)

    weave((0.0, process(0)), (SECOND, process(1)))
    weave((0.0, solve(2)))
    weave((0.0, solve(3)))
    for copy in started:
        copy.wait_send()


SECOND = 20.0
GATHER = ((9.0, 1.1), (5.0, 1.3))
ZPAIR, ZFAR, ZNEAR, ZLAST, ZRING, ZSHARE = 3.5, 6.5, 1.0, 5.0, 4.5, 2.0
PROD = 0.6
RS1, RS2, RS3, RS4 = (0.6, 1.2, 1.2, 1.2), (2.5, 1.2, 1.2, 1.2), (1.5, 0.7), 2.5
GM1, GM2, GM3 = (3.0, 2.0), (4.5, 3.0), (6.5, 6.0)
CHOL = 0.4


def power_step(slots, tiles, sketch):
    vmem = pl.BlockSpec(memory_space=pltpu.VMEM)
    return pl.pallas_call(
        power_kernel,
        name="power_step",
        out_shape=[jax.ShapeDtypeStruct((EDGE, K), F32), jax.ShapeDtypeStruct((K, K), F32)],
        in_specs=[pl.BlockSpec(memory_space=pltpu.SMEM), pl.BlockSpec(memory_space=pl.ANY), vmem],
        out_specs=[vmem, vmem],
        scratch_shapes=[
            pltpu.VMEM((EDGE, K), F32),
            pltpu.VMEM((GR[0], 128), F32),
            pltpu.VMEM((GR[1], 128), F32),
            pltpu.VMEM((128, 128), F32),
            pltpu.VMEM((4, 128, 128), F32),
            pltpu.VMEM((32, EDGE, EDGE), BF16),
            pltpu.VMEM((RB, EDGE, CB * EDGE), BF16),
            pltpu.VMEM((RB, K, EDGE), BF16),
            pltpu.VMEM((8, K, 128), F32),
            pltpu.VMEM((2, 8, 128, 128), F32),
            pltpu.VMEM((2, 8, 128, 128), F32),
            pltpu.VMEM((4, 1024, 128), BF16),
            pltpu.VMEM((2, RB, EDGE, EDGE), F32),
            pltpu.VMEM((2, 24, EDGE, 128), BF16),
            pltpu.VMEM((2, 24, EDGE, 128), BF16),
            pltpu.VMEM((2, 2, 4, EDGE, 128), F32),
            pltpu.VMEM((2, 12, 128, 128), F32),
            pltpu.VMEM((GR[0], 128), F32),
            pltpu.VMEM((GR[1], 128), F32),
            pltpu.VMEM((768, 128), F32),
            pltpu.VMEM((2, 2, 3, 64, 128), F32),
            pltpu.VMEM((2, 2, 3, 16, 128), F32),
            pltpu.VMEM((2, 32, 128), F32),
            pltpu.VMEM((2, 8, 32, 128), F32),
            pltpu.SemaphoreType.DMA,
            pltpu.SemaphoreType.DMA((320,)),
            pltpu.SemaphoreType.DMA((320,)),
        ],
        compiler_params=pltpu.CompilerParams(collective_id=0, has_side_effects=True, vmem_limit_bytes=60 << 20),
    )(slots, tiles, sketch)


def hand_kernel(basis, factor, basis_out, factor_out):
    basis_out[...] = basis[...]
    factor_out[...] = factor[...]


def hand_over(basis, factor):
    specs = [pl.BlockSpec((EDGE // 4, K), lambda n: (n, 0)), pl.BlockSpec((K // 4, K), lambda n: (n, 0))]
    return pl.pallas_call(
        hand_kernel,
        name="hand_over",
        grid=(4,),
        out_shape=[jax.ShapeDtypeStruct((EDGE, K), F32), jax.ShapeDtypeStruct((K, K), F32)],
        in_specs=specs,
        out_specs=specs,
        compiler_params=pltpu.CompilerParams(vmem_limit_bytes=60 << 20),
    )(basis, factor)


def local(tiles, tile_rows, tile_cols, counts, sketch):
    blocks = tiles[0, 0]
    slots = slot_table(tile_rows[0, 0], tile_cols[0, 0], counts[0, 0])
    return hand_over(*power_step(slots, blocks, sketch))


def solution(mesh):
    in_specs = (
        P("row", "blk", None, None, None),
        P("row", "blk", None),
        P("row", "blk", None),
        P("row", "blk"),
        P(("row", "blk"), None),
    )
    out_specs = (P(("row", "blk"), None), P())
    return jax.shard_map(local, mesh=mesh, in_specs=in_specs, out_specs=out_specs, check_vma=False)
```

```python
import functools
import jax
import jax.numpy as jnp
from jax import lax
from jax.experimental import pallas as pl
from jax.experimental.pallas import tpu as pltpu
from jax.sharding import PartitionSpec as P

F32 = jnp.float32
BF16 = jnp.bfloat16
MESH = pl.DeviceIdType.MESH
EDGE = 256
RB = 16
CB = 4
K = 512
PX, PY, PZ = 4, 4, 8


def where_am_i():
    row = lax.axis_index("row")
    blk = lax.axis_index("blk")
    return row // 2, row % 2, blk // PX, blk % PX


class Net:
    def __init__(self, send_sems, recv_sems):
        self.send_sems, self.recv_sems = send_sems, recv_sems
        self.used = 0
        self.z, self.c, self.y, self.x = where_am_i()

    def device(self, dz=0, dc=0, dy=0, dx=0):
        z = lax.rem(self.z + dz + PZ, PZ)
        c = 1 - self.c if dc else self.c
        y = lax.rem(self.y + dy + PY, PY)
        x = lax.rem(self.x + dx + PX, PX)
        return {"row": z * 2 + c, "blk": y * PX + x}

    def greet(self, steps):
        barrier = pltpu.get_barrier_semaphore()
        for step in steps:
            pl.semaphore_signal(barrier, inc=1, device_id=self.device(**step), device_id_type=MESH)
        pl.semaphore_wait(barrier, len(steps))

    def copy(self, src, dst, **step):
        slot = self.used
        self.used += 1
        return pltpu.make_async_remote_copy(
            src_ref=src, dst_ref=dst, send_sem=self.send_sems.at[slot], recv_sem=self.recv_sems.at[slot],
            device_id=self.device(**step), device_id_type=MESH)


NEIGHBOURS = [dict(dx=1), dict(dx=-1), dict(dy=1), dict(dy=-1), dict(dz=1), dict(dz=-1), dict(dc=1)]


def build_dense(slot_ref, tiles, dense):
    @pl.loop(0, RB)
    def _(i):
        for c in range(CB):
            slot = slot_ref[i * CB + c]
            keep = jnp.where(slot >= 0, 1.0, 0.0).astype(BF16)
            dense[i, :, c * EDGE:(c + 1) * EDGE] = tiles[jnp.maximum(slot, 0)] * keep


def slot_table(tile_rows, tile_cols, counts):
    slots = jnp.arange(tile_rows.shape[0], dtype=jnp.int32)
    spot = tile_rows * CB + tile_cols
    hit = (spot[None, :] == jnp.arange(RB * CB)[:, None]) & (slots < counts)[None, :]
    return jnp.max(jnp.where(hit, slots[None, :], -1), axis=1)


HIGH = lax.Precision.HIGHEST


def reach():
    steps = [dict(dc=1)]
    steps += [dict(dx=d) for d in (1, -1, 2)]
    steps += [dict(dy=d) for d in (1, -1, 2)]
    steps += [dict(dz=d) for d in (1, -1, 2, -2, 3, -3, 4)]
    return steps


PANELS = [(i, j) for j in range(4) for i in range(j + 1)]

GR = (512, 1024)


def lane(x, j):
    return jnp.take_along_axis(x, jnp.full(x.shape, j, jnp.int32), axis=1)


def sub(x, i):
    return jnp.broadcast_to(x[i:i + 1, :], x.shape)


def factor_block(S, E):
    rid = lax.broadcasted_iota(jnp.int32, (8, 128), 0)
    lid = lax.broadcasted_iota(jnp.int32, (8, 128), 1)
    E[:] = [(lid == rid + 8 * i).astype(F32) for i in range(16)]
    for g in range(16):
        cols = [lane(S[g], 8 * g + k) for k in range(8)]
        ss, ee = [sub(S[g], k) for k in range(8)], [sub(E[g], k) for k in range(8)]
        a = {(i, k): sub(cols[k], i) for k in range(8) for i in range(k, 8)}
        r, l, m = [None] * 8, {}, {}
        for k in range(8):
            r[k] = lax.rsqrt(a[k, k])
            for i in range(k + 1, 8):
                l[i, k] = a[i, k] * r[k]
            for i in range(k + 1, 8):
                for n in range(k + 1, i + 1):
                    a[i, n] = a[i, n] - l[i, k] * l[n, k]
            m[k, k] = r[k]
            for j in range(k):
                t = l[k, j] * m[j, j]
                for q in range(j + 1, k):
                    t = t + l[k, q] * m[q, j]
                m[k, j] = -(t * r[k])

        def mixed(terms, n):
            value = terms[0] * m[n, 0]
            for k in range(1, n + 1):
                value = value + terms[k] * m[n, k]
            return value

        us, es = [mixed(ss, n) for n in range(8)], [mixed(ee, n) for n in range(8)]
        later = {i: [lane(S[i], 8 * g + k) for k in range(8)] for i in range(g + 1, 16)}
        for i in range(g + 1, 16):
            for n in range(8):
                c = mixed(later[i], n)
                S[i] = S[i] - c * us[n]
                E[i] = E[i] - c * es[n]
        S[g], E[g] = us[0], es[0]
        for n in range(1, 8):
            S[g], E[g] = jnp.where(rid == n, us[n], S[g]), jnp.where(rid == n, es[n], E[g])
        yield CHOL
    S[:] = [jnp.where(lid >= rid + 8 * i, s, 0.0) for i, s in enumerate(S)]


def dot(a, b, dims=((1,), (0,))):
    return lax.dot_general(a, b, (dims, ((), ())), precision=HIGH, preferred_element_type=F32)


def weave(*works):
    queue = [[begin, n, work] for n, (begin, work) in enumerate(works)]
    while queue:
        entry = min(queue)
        try:
            entry[0] += next(entry[2])
        except StopIteration:
            queue.remove(entry)


def power_kernel(slot_ref, tiles_hbm, sketch_ref, basis, factor, image, gram0, gram1, S, inv, tiles, dense, gath, part, pair, chain, ci, acc, far, in1, sum2, in2,
                 gbuf0, gbuf1, gpair, g1, g2, gstage, gz, dma_sem, send_sems, recv_sems):
    net = Net(send_sems, recv_sems)
    load = pltpu.make_async_copy(tiles_hbm, tiles, dma_sem)
    load.start()
    mine = net.y * PX + net.x
    gath[mine] = sketch_ref[...].astype(F32).T.astype(BF16)
    net.greet(reach())
    started = []
    axes = [("dx", "dy"), ("dy", "dx")]

    def start(copy):
        copy.start()
        started.append(copy)
        return copy

    def begin(copy):
        copy.start()
        return copy

    def block_of(h, dp, dq):
        dx, dy = (dp, dq) if h == 0 else (dq, dp)
        return lax.rem(net.y + dy + PY, PY) * PX + lax.rem(net.x + dx + PX, PX)

    def slab(d):
        return lax.rem(net.z + d + PZ, PZ)

    def gather(t):
        base = 256 * t
        arrive = {}
        got = set()

        def go(h, dp, dq, axis, sign, key):
            where = gath.at[block_of(h, dp, dq), pl.ds(base + h * 128, 128), :]
            arrive[key] = net.used
            start(net.copy(where, where, **{axis: sign}))

        def received(h, dp, dq):
            where = gath.at[block_of(h, dp, dq), pl.ds(base + h * 128, 128), :]
            n = arrive[h, dp, dq]
            pltpu.make_async_remote_copy(
                src_ref=where, dst_ref=where, send_sem=send_sems.at[n], recv_sem=recv_sems.at[n],
                device_id=net.device(dx=1), device_id_type=MESH).wait_recv()

        def multiply(dx, dy):
            i = block_of(0, dx, dy)
            block = gath[i, base:base + 256, :]
            for c in range(CB):
                prod = jnp.dot(block, dense[i, :, c * EDGE:(c + 1) * EDGE], preferred_element_type=F32)
                for s in range(2):
                    piece = prod[:, s * 128:(s + 1) * 128]
                    if (dx, dy) == (0, 0):
                        part[2 * c + s, base:base + 256, :] = piece
                    else:
                        part[2 * c + s, base:base + 256, :] += piece

        for h in range(2):
            p, q = axes[h]
            go(h, 0, 0, p, 1, (h, -1, 0))
            go(h, 0, 0, p, -1, (h, 1, 0))
        for h in range(2):
            p, q = axes[h]
            go(h, 0, 0, q, 1, (h, 0, -1))
            go(h, 0, 0, q, -1, (h, 0, 1))
        if t == 0:
            load.wait()
            build_dense(slot_ref, tiles, dense)
        yield GATHER[t][0]
        multiply(0, 0)
        order = [(-1, 0), (1, 0), (0, -1), (0, 1), (2, 0), (-1, -1), (-1, 1), (0, 2), (1, -1), (1, 1), (-1, 2), (2, -1), (2, 1), (1, 2), (2, 2)]
        for dp, dq in order:
            for h in range(2):
                p, q = axes[h]
                received(h, dp, dq)
                if dq == 0:
                    if dp == -1:
                        go(h, dp, 0, p, 1, (h, 2, 0))
                    go(h, dp, 0, q, 1, (h, dp, -1))
                    go(h, dp, 0, q, -1, (h, dp, 1))
                elif dq == -1 and dp in (0, 2):
                    go(h, dp, dq, q, 1, (h, dp, 2))
                elif dq == 1 and dp in (-1, 1):
                    go(h, dp, dq, q, -1, (h, dp, 2))
            got.add((dp, dq))
            if (dq, dp) in got:
                for dx, dy in {(dp, dq): 0, (dq, dp): 0}:
                    multiply(dx, dy)
            yield GATHER[t][1]

    def columns(t):
        base = 256 * t
        own = pl.multiple_of(base + net.c * 128, 128)
        other = pl.multiple_of(base + (1 - net.c) * 128, 128)
        pairs, legs, shared = {}, {}, []

        def merge(d):
            pairs[d].wait_recv()
            part[slab(d), pl.ds(own, 128), :] += pair[t, slab(d)]

        def leg(name, d, u, slot, dz):
            src = part.at[slab(d), pl.ds(own, 128) if u is None else pl.ds(pl.multiple_of(own + u * 64, 64), 64), :]
            dst = chain.at[t, slot] if u is None else chain.at[t, slot, pl.ds(0, 64), :]
            legs[name] = start(net.copy(src, dst, dz=dz))

        for d in (4, 3, -3, 1, -1, 2, -2, 0):
            pairs[d] = start(net.copy(part.at[slab(d), pl.ds(other, 128), :], pair.at[t, slab(d)], dc=1))
        yield ZPAIR
        merge(4)
        leg((4, 1), 4, 0, 0, 2)
        leg((4, -1), 4, 1, 1, -2)
        merge(3)
        leg((3, 1), 3, None, 2, 1)
        merge(-3)
        leg((3, -1), -3, None, 3, -1)
        merge(1)
        leg((1, 1), 1, None, 4, 1)
        merge(-1)
        leg((1, -1), -1, None, 5, -1)
        merge(2)
        merge(-2)
        yield ZFAR
        for n, sign in enumerate((1, -1)):
            legs[3, sign].wait_recv()
            part[slab(2 * sign), pl.ds(own, 128), :] += chain[t, 2 + n]
            legs[4, sign].wait_recv()
            part[slab(2 * sign), pl.ds(pl.multiple_of(own + n * 64, 64), 64), :] += chain[t, n, 0:64, :]
            leg((2, sign), 2 * sign, None, 6 + n, 2 * sign)
        merge(0)
        yield ZNEAR
        value = part[net.z, pl.ds(own, 128), :]
        for n, sign in enumerate((1, -1)):
            legs[1, sign].wait_recv()
            value = value + chain[t, 4 + n]
        yield ZLAST
        for n, sign in enumerate((1, -1)):
            legs[2, sign].wait_recv()
            value = value + chain[t, 6 + n]

        def place(d, u=None):
            at = slab(d) * 128 + (0 if u is None else u * 64)
            return ci.at[2 * t + net.c, pl.ds(pl.multiple_of(at, 64), 128 if u is None else 64), :]

        def send(d, dz, u=None):
            return start(net.copy(place(d, u), place(d, u), dz=dz))

        def share(d, u=None):
            shared.append(start(net.copy(place(d, u), place(d, u), dc=1)))

        ci[2 * t + net.c, pl.ds(pl.multiple_of(net.z * 128, 128), 128), :] = value.T.astype(BF16)
        two = {sign: send(0, 2 * sign) for sign in (1, -1)}
        one = {sign: send(0, sign) for sign in (1, -1)}
        share(0)
        yield ZRING
        three, four = {}, {}
        for n, sign in enumerate((1, -1)):
            two[sign].wait_recv()
            four[sign] = send(-2 * sign, 2 * sign, n)
            three[sign] = send(-2 * sign, sign)
            share(-2 * sign)
        for sign in (1, -1):
            one[sign].wait_recv()
            share(-sign)
        yield ZRING
        for sign in (1, -1):
            three[sign].wait_recv()
            share(-3 * sign)
        for n, sign in enumerate((1, -1)):
            four[sign].wait_recv()
            share(4, n)
        yield ZSHARE
        for copy in shared:
            copy.wait_recv()

    def rows_out(t):
        moves, moves2, made = {}, {}, set()
        QS = (2, 1, -1, 0)

        def product(h, dp, dq):
            spot = (dp, dq) if h == 0 else (dq, dp)
            i = block_of(h, dp, dq)
            if spot not in made:
                made.add(spot)
                right = jnp.concatenate([ci[2 * t], ci[2 * t + 1]], axis=1)
                acc[t, i] = jnp.dot(dense[i], right, preferred_element_type=F32)
            return acc[t, i, :, h * 128:(h + 1) * 128]

        def send1(h, dp, dq, sign, value):
            n = len(moves)
            far[t, n] = value.astype(BF16)
            moves[h, dp, dq] = start(net.copy(far.at[t, n], in1.at[t, n], **{axes[h][0]: sign})), n

        def via(dq):
            return 1 if dq in (0, 2) else -1

        def send2(h, dq, piece, sign):
            n = len(moves2)
            moves2[h, dq, piece] = start(net.copy(sum2.at[t, h, dq % 4, pl.ds(piece * 128, 128), :], in2.at[t, n], **{axes[h][1]: sign})), n

        for dq in QS:
            for h in range(2):
                send1(h, 2, dq, via(dq), product(h, 2, dq))
            yield PROD
        for dq in QS:
            for h in range(2):
                s = -via(dq)
                send1(h, s, dq, s, product(h, s, dq))
            yield PROD
        for dq in QS:
            for h in range(2):
                product(h, via(dq), dq)
                product(h, 0, dq)
            yield RS1[QS.index(dq)]
            for h in range(2):
                s = via(dq)
                copy, n = moves[h, 2, dq]
                copy.wait_recv()
                send1(h, s, dq, s, product(h, s, dq) + in1[t, n].astype(F32))
        for dq in QS:
            yield RS2[QS.index(dq)]
            for h in range(2):
                value = product(h, 0, dq)
                for s in (-via(dq), via(dq)):
                    copy, n = moves[h, s, dq]
                    copy.wait_recv()
                    value = value + in1[t, n].astype(F32)
                sum2[t, h, dq % 4] = value
                if dq == 2:
                    send2(h, 2, 0, 1)
                    send2(h, 2, 1, -1)
                elif dq != 0:
                    send2(h, dq, 0 if dq == -1 else 1, dq)
        for dq in (1, -1):
            yield RS3[dq == -1]
            for h in range(2):
                through = 0 if dq == 1 else 1
                copy, n = moves2[h, 2, through]
                copy.wait_recv()
                sum2[t, h, dq % 4, through * 128:(through + 1) * 128, :] += in2[t, n]
                send2(h, dq, through, dq)
        yield RS4
        for h in range(2):
            for piece in range(2):
                value = sum2[t, h, 0, piece * 128:(piece + 1) * 128, :]
                for dq in (1, -1):
                    copy, n = moves2[h, dq, piece]
                    copy.wait_recv()
                    value = value + in2[t, n]
                image[piece * 128:(piece + 1) * 128, t * 256 + h * 128:t * 256 + (h + 1) * 128] = value

    def moments(t):
        size = GR[t]
        gbuf, out = (gbuf0, gram0) if t == 0 else (gbuf1, gram1)
        scale = 1.0 / (lax.axis_size("row") * lax.axis_size("blk") * EDGE)
        panels = [p for p in PANELS if p[1] // 2 == t]
        for n, (i, j) in enumerate(panels):
            gbuf[n * 128:(n + 1) * 128, :] = lax.dot_general(
                image[:, i * 128:(i + 1) * 128], image[:, j * 128:(j + 1) * 128], (((0,), (0,)), ((), ())),
                precision=HIGH, preferred_element_type=F32) * scale
        gbuf[size - 128:, :] = jnp.zeros((128, 128), F32)
        half, quarter, first, second = size // 2, size // 4, size // 16, size // 64
        base = pl.multiple_of(net.c * half, 256)
        twin = start(net.copy(gbuf.at[pl.ds(pl.multiple_of((1 - net.c) * half, 256), half), :], gpair.at[pl.ds(t * 256, half), :], dc=1))
        yield GM1[t]
        twin.wait_recv()
        gbuf[pl.ds(base, half), :] += gpair[t * 256:t * 256 + half, :]

        def cut(at, pos, d, step):
            return pl.ds(pl.multiple_of(at + lax.rem(pos + d + 4, 4) * step, 8), step)

        place = (net.x, net.y)
        ats = [base + v * quarter for v in range(2)]
        for level, step in enumerate((first, second)):
            copies = {}
            for d in (2, 1, -1):
                for v in range(2):
                    n = {2: 0, 1: 1, -1: 2}[d]
                    land = g1.at[t, v, n, pl.ds(0, step), :] if level == 0 else g2.at[t, v, n, pl.ds(0, step), :]
                    axis = axes[v][level]
                    copies[v, n] = start(net.copy(gbuf.at[cut(ats[v], place[(v + level) % 2], d, step), :], land, **{axis: d}))
            yield GM2[t]
            for v in range(2):
                here = cut(ats[v], place[(v + level) % 2], 0, step)
                value = gbuf[here, :]
                for n in range(3):
                    copies[v, n].wait_recv()
                    value = value + (g1 if level == 0 else g2)[t, v, n, 0:step, :]
                if level == 0:
                    gbuf[here, :] = value
                else:
                    gstage[t, v * second:(v + 1) * second, :] = value
                ats[v] = pl.multiple_of(ats[v] + place[(v + level) % 2] * step, 8)
        both = 2 * second
        offsets = (4, 3, -3, 2, -2, 1, -1, 0)
        copies = [start(net.copy(gstage.at[t, pl.ds(0, both), :], gz.at[t, n, pl.ds(0, both), :], dz=d)) for n, d in enumerate(offsets[:-1])]
        gz[t, 7, 0:both, :] = gstage[t, 0:both, :]
        yield GM3[t]
        for copy in copies:
            copy.wait_recv()
        value = None
        for spot in range(PZ):
            d = lax.rem(net.z - spot + PZ, PZ)
            at = 0
            for n, o in enumerate(offsets):
                at = at + jnp.where(d == o % PZ, n, 0)
            term = gz[t, at, 0:both, :]
            value = term if value is None else value + term
        for v in range(2):
            out[pl.ds(ats[v], second), :] = value[v * second:(v + 1) * second, :]
        for level, step in ((1, second), (0, first)):
            copies = []
            for v in range(2):
                if level == 0:
                    ats[v] = base + v * quarter + place[v % 2] * first
                where = out.at[pl.ds(pl.multiple_of(ats[v], 8), step), :]
                for d in (2, 1, -1):
                    copies.append(start(net.copy(where, where, **{axes[v][level]: d})))
            yield GM2[t]
            for copy in copies:
                copy.wait_recv()
        where = out.at[pl.ds(base, half), :]
        twin = start(net.copy(where, where, dc=1))
        yield GM1[t]
        twin.wait_recv()

    index = {p: n for n, p in enumerate(PANELS)}

    def span(b):
        return slice(b * 128, (b + 1) * 128)

    def panel(i, j):
        n = index[i, j]
        return gram0[span(n), :] if n < 3 else gram1[span(n - 3), :]

    def reduced(i, j, upto):
        value = panel(i, j)
        for k in range(upto):
            value = value - dot(factor[span(k), span(i)], factor[span(k), span(j)], ((0,), (0,)))
        return value

    def solve(b):
        for i in range(b):
            factor[span(b), span(i)] = jnp.zeros((128, 128), F32)
        if b == 2:
            for j in (2, 3):
                for i in (0, 1):
                    factor[span(i), span(j)] = dot(inv[i], reduced(i, j, i))
        yield CHOL
        S[...] = reduced(b, b, b)
        value = image[:, span(b)]
        for k in range(b):
            value = value - dot(basis[:, span(k)], factor[span(k), span(b)])
        yield CHOL
        rows, e = [S[8 * g:8 * g + 8, :] for g in range(16)], []
        yield from factor_block(rows, e)
        for g in range(16):
            factor[b * 128 + 8 * g:b * 128 + 8 * g + 8, span(b)] = rows[g]
            inv[b, 8 * g:8 * g + 8, :] = e[g]
        yield CHOL
        if b % 2 == 0:
            factor[span(b), span(b + 1)] = dot(inv[b], reduced(b, b + 1, b))
        yield CHOL
        basis[:, span(b)] = dot(value, inv[b], ((1,), (1,)))

    def process(t):
        yield from gather(t)
        yield from columns(t)
        yield from rows_out(t)
        yield from moments(t)

        if t == 0:
            yield from solve(0)
            yield from solve(1)

    weave((0.0, process(0)), (SECOND, process(1)))
    weave((0.0, solve(2)))
    weave((0.0, solve(3)))
    for copy in started:
        copy.wait_send()


SECOND = 23.0
GATHER = ((9.0, 1.1), (5.0, 1.3))
ZPAIR, ZFAR, ZNEAR, ZLAST, ZRING, ZSHARE = 3.5, 6.5, 1.0, 5.0, 4.5, 2.0
PROD = 0.6
RS1, RS2, RS3, RS4 = (0.6, 1.2, 1.2, 1.2), (2.5, 1.2, 1.2, 1.2), (1.5, 0.7), 2.5
GM1, GM2, GM3 = (3.0, 2.0), (4.5, 3.0), (6.5, 6.0)
CHOL = 0.4


def power_step(slots, tiles, sketch):
    vmem = pl.BlockSpec(memory_space=pltpu.VMEM)
    return pl.pallas_call(
        power_kernel,
        name="power_step",
        out_shape=[jax.ShapeDtypeStruct((EDGE, K), F32), jax.ShapeDtypeStruct((K, K), F32)],
        in_specs=[pl.BlockSpec(memory_space=pltpu.SMEM), pl.BlockSpec(memory_space=pl.ANY), vmem],
        out_specs=[vmem, vmem],
        scratch_shapes=[
            pltpu.VMEM((EDGE, K), F32),
            pltpu.VMEM((GR[0], 128), F32),
            pltpu.VMEM((GR[1], 128), F32),
            pltpu.VMEM((128, 128), F32),
            pltpu.VMEM((4, 128, 128), F32),
            pltpu.VMEM((32, EDGE, EDGE), BF16),
            pltpu.VMEM((RB, EDGE, CB * EDGE), BF16),
            pltpu.VMEM((RB, K, EDGE), BF16),
            pltpu.VMEM((8, K, 128), F32),
            pltpu.VMEM((2, 8, 128, 128), F32),
            pltpu.VMEM((2, 8, 128, 128), F32),
            pltpu.VMEM((4, 1024, 128), BF16),
            pltpu.VMEM((2, RB, EDGE, EDGE), F32),
            pltpu.VMEM((2, 24, EDGE, 128), BF16),
            pltpu.VMEM((2, 24, EDGE, 128), BF16),
            pltpu.VMEM((2, 2, 4, EDGE, 128), F32),
            pltpu.VMEM((2, 12, 128, 128), F32),
            pltpu.VMEM((GR[0], 128), F32),
            pltpu.VMEM((GR[1], 128), F32),
            pltpu.VMEM((768, 128), F32),
            pltpu.VMEM((2, 2, 3, 64, 128), F32),
            pltpu.VMEM((2, 2, 3, 16, 128), F32),
            pltpu.VMEM((2, 32, 128), F32),
            pltpu.VMEM((2, 8, 32, 128), F32),
            pltpu.SemaphoreType.DMA,
            pltpu.SemaphoreType.DMA((320,)),
            pltpu.SemaphoreType.DMA((320,)),
        ],
        compiler_params=pltpu.CompilerParams(collective_id=0, has_side_effects=True, vmem_limit_bytes=60 << 20),
    )(slots, tiles, sketch)


def hand_kernel(basis, factor, basis_out, factor_out):
    basis_out[...] = basis[...]
    factor_out[...] = factor[...]


def hand_over(basis, factor):
    specs = [pl.BlockSpec((EDGE // 4, K), lambda n: (n, 0)), pl.BlockSpec((K // 4, K), lambda n: (n, 0))]
    return pl.pallas_call(
        hand_kernel,
        name="hand_over",
        grid=(4,),
        out_shape=[jax.ShapeDtypeStruct((EDGE, K), F32), jax.ShapeDtypeStruct((K, K), F32)],
        in_specs=specs,
        out_specs=specs,
        compiler_params=pltpu.CompilerParams(vmem_limit_bytes=60 << 20),
    )(basis, factor)


def local(tiles, tile_rows, tile_cols, counts, sketch):
    blocks = tiles[0, 0]
    slots = slot_table(tile_rows[0, 0], tile_cols[0, 0], counts[0, 0])
    return hand_over(*power_step(slots, blocks, sketch))


def solution(mesh):
    in_specs = (
        P("row", "blk", None, None, None),
        P("row", "blk", None),
        P("row", "blk", None),
        P("row", "blk"),
        P(("row", "blk"), None),
    )
    out_specs = (P(("row", "blk"), None), P())
    return jax.shard_map(local, mesh=mesh, in_specs=in_specs, out_specs=out_specs, check_vma=False)
```
